32 devices in a mesh: row: 16 (over z, y, core), col: 2 (over x).
Axes of the slice: x: 2, y: 2, z: 4, core: 2. Of those that a mesh axis runs over, the one named last changes fastest.
Arguments:
- velocity: float32 [3, 16, 1024, 1024], P(None, None, 'row', 'col'), may hold values from -6 to 6
- dy_op: bfloat16 [1024, 1024], replicated, may hold values from -0.1875 to 0.1875
- dz_op: bfloat16 [1024, 1024], replicated, may hold values from -0.1875 to 0.1875
- node_force: float32 [3, 256], P(None, ('row', 'col')), may hold values from -6 to 6
- node_cell: int32 [3, 256], P(None, ('row', 'col')), may hold values from 0 to 1023, as said below
Outputs:
- tendency: float32 [3, 16, 1024, 1024], P(None, None, 'row', 'col')
The draws below stay inside these ranges and needn't reach their ends.
Inputs may be any that keep to these rules, and one draw needn't show every extreme that they name: `node_cell`: the nodes of the block held by device (r, c) of the mesh have their z coordinate in the c-th of the 2 equal ranges of z; x lies below 16, y below 1024.
All inputs are finite; a program needn't handle non-finite values.
Results may differ from the reference program's by a relative error of at most 0.0029.
Values sent between devices are 32-bit elements; how exact they have to be, the bound alone decides.
No kernel may reach another device: no remote copies, remote signals or barrier semaphores. Data moves between devices by JAX's collectives and lax.ppermute only.
A program may use at most 384 MiB of HBM per device.

```python
import jax
import jax.numpy as jnp
from jax import lax

NY = 1024
NZ = 1024
NODE_DEV = 8
NX = 16
NODES = 256
N_ROW = 16
N_COL = 2


def draw_node_cell(key, part):
    keys = jax.random.split(key, 3)
    total = NODE_DEV * N_ROW * N_COL
    counter = jnp.arange(total, dtype=jnp.int32)
    block_id = counter // NODE_DEV
    slot_id = counter % NODE_DEV
    col_of = block_id % N_COL
    span = NZ // N_COL
    x_cells = jax.random.randint(keys[0], (total,), 0, NX)
    x_cells = jnp.where(slot_id == 0, 0, x_cells)
    y_cells = jax.random.randint(keys[1], (total,), 0, NY)
    z_cells = col_of * span + jax.random.randint(keys[2], (total,), 0, span)
    z_cells = jnp.where(slot_id == NODE_DEV - 1, col_of * span + span - 1, z_cells)
    return jnp.stack([x_cells, y_cells, z_cells]).astype(jnp.int32)


def shard_levels(rng, extent, cuts, low, top_value):
    gain, own = 1.0, jax.random.fold_in(rng, 6)
    for position, parts in cuts:
        heights = jnp.exp(jax.random.uniform(jax.random.fold_in(own, position), (parts,), jnp.float32, low / len(cuts), top_value / len(cuts)))
        gain = gain * jnp.repeat(heights, extent[position] // parts).reshape([-1 if axis == position else 1 for axis in range(len(extent))])
    return gain


def noise(rng, dims, width, reach, cuts=(), held_as=jnp.bfloat16):
    entries = jax.random.normal(rng, dims, jnp.float32) * width
    if len(cuts) > 0:
        entries = shard_levels(rng, dims, cuts, -0.22, 0.18) * entries
    return jnp.clip(entries, min=-reach, max=reach).astype(held_as)


def setup_inputs(seed: int = 0) -> dict:
    arg_keys = jax.random.split(jax.random.key(seed), 6)
    return {
        "velocity": noise(arg_keys[0], (3, NX, NY, NZ), 1.0, 6.0, ((2, 16), (3, 2)), jnp.float32),
        "dy_op": noise(arg_keys[1], (NY, NY), NY ** -0.5, 0.1875),
        "dz_op": noise(arg_keys[2], (NZ, NZ), NZ ** -0.5, 0.1875),
        "node_force": noise(arg_keys[3], (3, NODES), 1.0, 6.0, ((1, 32),), jnp.float32),
        "node_cell": draw_node_cell(jax.random.fold_in(arg_keys[5], 71), 0),
    }


def reference(velocity, dy_op, dz_op, node_force, node_cell):
    coarse = lax.optimization_barrier(velocity.astype(jnp.bfloat16)).astype(jnp.float32)
    dy_full = dy_op.astype(jnp.float32)
    full_z_derivative = dz_op.astype(jnp.float32)

    def one_plane(both_parts):
        exact_f, coarse_f = both_parts
        gradient_in_y = jnp.einsum('ab,cbz->caz', dy_full, coarse_f)
        gradient_in_z = jnp.einsum('cyb,ab->cya', coarse_f, full_z_derivative)
        return -(exact_f[1][None] * gradient_in_y + exact_f[2][None] * gradient_in_z)

    planes = lax.map(one_plane, (jnp.moveaxis(velocity, 1, 0), jnp.moveaxis(coarse, 1, 0)))
    tendency = jnp.moveaxis(planes, 0, 1)
    flat_index = ((node_cell[0] * NY + node_cell[1]) * NZ + node_cell[2]).astype(jnp.int32)
    summed = tendency.reshape(3, -1).at[:, flat_index].add(node_force)
    return summed.reshape(tendency.shape)
```

```python
import functools

import jax
import jax.numpy as jnp
from jax import lax
from jax.experimental import pallas as pl
from jax.experimental.pallas import tpu as pltpu
from jax.sharding import PartitionSpec as P

VMEM = 60 << 20
CHUNKS = ((0, 2), (2, 1))
SHARES = (6, 2, 4)
NODE_STEPS = (2, 2)


def y_kernel(op_ref, lines_ref, grad_ref):
    shape = lines_ref.shape
    lines = lines_ref[...].reshape(shape[0] * shape[3], shape[4]).astype(jnp.bfloat16)
    grad = jnp.dot(op_ref[...], lines, preferred_element_type=jnp.float32)
    grad_ref[...] = grad.reshape(shape)


def y_gradient(op, lines):
    rows, comps, planes, height, width = lines.shape
    tile = min(width, 256)
    block = pl.BlockSpec((rows, 1, 1, height, tile), lambda c, p, j: (0, c, p, 0, j))
    flops = 2 * op.shape[0] * op.shape[1] * comps * planes * width
    return pl.pallas_call(
        y_kernel,
        grid=(comps, planes, width // tile),
        in_specs=[pl.BlockSpec(op.shape, lambda c, p, j: (0, 0)), block],
        out_specs=block,
        out_shape=jax.ShapeDtypeStruct(lines.shape, jnp.float32),
        compiler_params=pltpu.CompilerParams(vmem_limit_bytes=VMEM),
        cost_estimate=pl.CostEstimate(
            flops=flops, bytes_accessed=8 * lines.size + 2 * op.size, transcendentals=0
        ),
        name="y_gradient",
    )(op, lines)


def in_place(kernel, out, shape, name, grid, args, specs, out_spec, flops, size):
    kept = [] if out is None else [out]
    return pl.pallas_call(
        kernel,
        grid=grid,
        in_specs=specs + [pl.BlockSpec(memory_space=pl.ANY)] * len(kept),
        out_specs=out_spec,
        out_shape=jax.ShapeDtypeStruct(shape, jnp.float32),
        input_output_aliases={len(specs): 0} if kept else {},
        compiler_params=pltpu.CompilerParams(vmem_limit_bytes=VMEM),
        cost_estimate=pl.CostEstimate(flops=flops, bytes_accessed=size, transcendentals=0),
        name=name,
    )(*args, *kept)


def z_kernel(n_blocks, carrier_ref, *refs):
    field_refs, op_refs, out_ref = refs[:n_blocks], refs[n_blocks : 2 * n_blocks], refs[-1]
    planes, height, width = out_ref.shape
    grad = None
    for field_ref, op_ref in zip(field_refs, op_refs):
        field = field_ref[...].reshape(planes * height, width).astype(jnp.bfloat16)
        part = lax.dot_general(
            field, op_ref[...], (((1,), (1,)), ((), ())), preferred_element_type=jnp.float32
        )
        grad = part if grad is None else grad + part
    out_ref[...] = -(carrier_ref[...] * grad.reshape(out_ref.shape))


def z_terms(out, flat, planes, start, others, ops):
    count, height, width = others[0].shape if others else flat.shape
    tile = 4
    first, cycle, carried = start // tile, planes // tile, 2 * planes // tile
    here = pl.BlockSpec((tile, height, width), lambda i: (first + i, 0, 0))
    carrier = pl.BlockSpec((tile, height, width), lambda i: (carried + (first + i) % cycle, 0, 0))
    field = pl.BlockSpec((tile, height, width), lambda i: (i, 0, 0))
    op = pl.BlockSpec((width, width), lambda i: (0, 0))
    size = count * height * width
    return in_place(
        functools.partial(z_kernel, 1 + len(others)),
        out,
        flat.shape,
        "z_terms",
        (count // tile,),
        [flat, flat, *others, *ops],
        [carrier, here] + [field] * len(others) + [op] * len(ops),
        here,
        2 * size * width * len(ops),
        4 * size * (2 + len(ops)),
    )


def node_kernel(planes, node_ref, force_ref, base_ref, out_ref):
    tile, height, width = out_ref.shape
    out_ref[...] = base_ref[...]
    lane = lax.broadcasted_iota(jnp.int32, (1, width), 1)
    start = pl.program_id(0) * tile
    comp, begin = start // planes, start % planes

    def add_node(n, _):
        x, y, z = node_ref[0, n] - begin, node_ref[1, n], node_ref[2, n]

        @pl.when((x >= 0) & (x < tile) & (y >= 0) & (y < height) & (z >= 0) & (z < width))
        def _():
            row = out_ref[x, pl.ds(y, 1), :]
            out_ref[x, pl.ds(y, 1), :] = row + jnp.where(lane == z, force_ref[comp, n], 0.0)

        return 0

    lax.fori_loop(0, node_ref.shape[1], add_node, 0)


def add_nodes(out, planes, nodes, forces):
    total, height, width = out.shape
    tile = planes // 2
    block = pl.BlockSpec((tile, height, width), lambda i: (i, 0, 0))
    smem = pl.BlockSpec(memory_space=pltpu.SMEM)
    return pl.pallas_call(
        functools.partial(node_kernel, planes),
        grid=(total // tile,),
        in_specs=[smem, smem, block],
        out_specs=block,
        out_shape=jax.ShapeDtypeStruct(out.shape, jnp.float32),
        input_output_aliases={2: 0},
        compiler_params=pltpu.CompilerParams(vmem_limit_bytes=VMEM),
        cost_estimate=pl.CostEstimate(flops=out.size, bytes_accessed=8 * out.size, transcendentals=0),
        name="add_nodes",
    )(nodes, forces, out)


def combine_kernel(base_ref, carrier_ref, grad_ref, out_ref):
    out_ref[...] = base_ref[...] - carrier_ref[...] * grad_ref[:, 0]


def combine(out, flat, planes, grad, start):
    total, height, width = out.shape
    comps = grad.shape[1]
    tile = planes // 4
    per = planes // tile
    first = start * per
    here = pl.BlockSpec((tile, height, width), lambda c, i: (first + c * per + i, 0, 0))
    carrier = pl.BlockSpec((tile, height, width), lambda c, i: (per + i, 0, 0))
    return pl.pallas_call(
        combine_kernel,
        grid=(comps, per),
        in_specs=[here, carrier, pl.BlockSpec((tile, 1, height, width), lambda c, i: (i, c, 0, 0))],
        out_specs=here,
        out_shape=jax.ShapeDtypeStruct(out.shape, jnp.float32),
        input_output_aliases={0: 0},
        compiler_params=pltpu.CompilerParams(vmem_limit_bytes=VMEM),
        cost_estimate=pl.CostEstimate(
            flops=2 * grad.size, bytes_accessed=16 * grad.size, transcendentals=0
        ),
        name="combine",
    )(out, flat, grad)


def solution(mesh):
    n_row, n_col = mesh.shape["row"], mesh.shape["col"]

    def exchange(block):
        return lax.all_to_all(block, "row", split_axis=0, concat_axis=0, tiled=True)

    def per_device(velocity, dy_op, dz_op, node_force, node_cell):
        comps, planes, height, width = velocity.shape
        row_pos, col_pos = lax.axis_index("row"), lax.axis_index("col")
        total = comps * planes
        n_chunks = len(CHUNKS)
        n_phases = 2 * n_chunks

        def gather_step(known, step):
            moved = lax.ppermute(known, "row", [(i, i ^ step) for i in range(n_row)])
            return jnp.concatenate([known, moved], axis=1)

        def chunk_of(velocity, k):
            first, count = CHUNKS[k]
            block = velocity[first : first + count].swapaxes(0, 1)
            return block.reshape(n_row, planes // n_row, count, height, width).swapaxes(1, 2)

        def piece_of(velocity, k):
            unit = total // sum(SHARES)
            begin, end = unit * sum(SHARES[:k]), unit * sum(SHARES[: k + 1])
            return velocity.reshape(total, height, width)[begin:end]

        own_rows = lax.dynamic_slice_in_dim(dz_op, col_pos * width, width, 0)
        ops = [
            lax.dynamic_slice_in_dim(own_rows, (col_pos + s) % n_col * width, width, 1)
            for s in range(n_col)
        ]
        known = jnp.concatenate([node_force, node_cell.astype(jnp.float32)])
        steps = [1 << k for k in range(n_row.bit_length() - 1)][::-1]

        chunks = [chunk_of(velocity, 0)]
        pieces = [piece_of(velocity, 0)]
        grads = [None] * n_chunks
        out, start = None, 0
        for phase in range(n_phases):
            moved = exchange(chunks[phase])
            others = None
            if phase < len(SHARES):
                others = [
                    lax.ppermute(pieces[phase], "col", [(i, (i - s) % n_col) for i in range(n_col)])
                    for s in range(1, n_col)
                ]
            if phase < len(NODE_STEPS):
                last = phase == len(NODE_STEPS) - 1
                for _ in range(len(steps) if last else NODE_STEPS[phase]):
                    known = gather_step(known, steps.pop(0))
            if phase + 1 < n_chunks:
                chunks.append(chunk_of(velocity, phase + 1))
            if phase + 1 < len(SHARES):
                pieces.append(piece_of(velocity, phase + 1))
            if 1 <= phase <= n_chunks:
                chunks.append(y_gradient(dy_op, arrived))
            if phase > 0 and start < total:
                flat = velocity.reshape(total, height, width)
                out = z_terms(out, flat, planes, start, arriving, ops)
                start += arriving[0].shape[0]
            if phase == n_phases - 1:
                break
            arrived, arriving = moved, others
            if phase >= n_chunks:
                grads[phase - n_chunks] = moved
            state = velocity, chunks, pieces, arrived, arriving, grads, out, known
            state = lax.optimization_barrier(state)
            velocity, chunks, pieces, arrived, arriving, grads, out, known = state
        grads[-1] = moved
        flat = velocity.reshape(total, height, width)
        origin = jnp.stack([0 * row_pos, row_pos * height, col_pos * width])
        cells = known[comps:].astype(jnp.int32) - origin[:, None].astype(jnp.int32)
        out = add_nodes(out, planes, cells, known[:comps])
        for (first, count), grad in zip(CHUNKS, grads):
            grad = grad.swapaxes(1, 2).reshape(planes, count, height, width)
            out = combine(out, flat, planes, grad, first)
        return out.reshape(velocity.shape)

    return jax.shard_map(
        per_device,
        mesh=mesh,
        in_specs=(
            P(None, None, "row", "col"),
            P(),
            P(),
            P(None, ("row", "col")),
            P(None, ("row", "col")),
        ),
        out_specs=P(None, None, "row", "col"),
        check_vma=False,
    )
```

```python
import functools

import jax
import jax.numpy as jnp
from jax import lax
from jax.experimental import pallas as pl
from jax.experimental.pallas import tpu as pltpu
from jax.sharding import PartitionSpec as P

VMEM = 60 << 20
GROUP = 4


def y_kernel(op_ref, lines_ref, grad_ref):
    shape = lines_ref.shape
    lines = lines_ref[...].reshape(shape[0] * shape[3], shape[4]).astype(jnp.bfloat16)
    grad = jnp.dot(op_ref[...], lines, preferred_element_type=jnp.float32)
    grad_ref[...] = grad.reshape(shape)


def y_gradient(op, lines):
    rows, comps, planes, height, width = lines.shape
    tile = min(width, 256)
    block = pl.BlockSpec((rows, 1, 1, height, tile), lambda c, p, j: (0, c, p, 0, j))
    flops = 2 * op.shape[0] * op.shape[1] * comps * planes * width
    return pl.pallas_call(
        y_kernel,
        grid=(comps, planes, width // tile),
        in_specs=[pl.BlockSpec(op.shape, lambda c, p, j: (0, 0)), block],
        out_specs=block,
        out_shape=jax.ShapeDtypeStruct(lines.shape, jnp.float32),
        compiler_params=pltpu.CompilerParams(vmem_limit_bytes=VMEM),
        cost_estimate=pl.CostEstimate(
            flops=flops, bytes_accessed=8 * lines.size + 2 * op.size, transcendentals=0
        ),
        name="y_gradient",
    )(op, lines)


def in_place(kernel, out, shape, name, grid, args, specs, out_spec, flops, size):
    kept = [] if out is None else [out]
    return pl.pallas_call(
        kernel,
        grid=grid,
        in_specs=specs + [pl.BlockSpec(memory_space=pl.ANY)] * len(kept),
        out_specs=out_spec,
        out_shape=jax.ShapeDtypeStruct(shape, jnp.float32),
        input_output_aliases={len(specs): 0} if kept else {},
        compiler_params=pltpu.CompilerParams(vmem_limit_bytes=VMEM),
        cost_estimate=pl.CostEstimate(flops=flops, bytes_accessed=size, transcendentals=0),
        name=name,
    )(*args, *kept)


def z_kernel(n_blocks, carrier_ref, *refs):
    field_refs, op_refs, out_ref = refs[:n_blocks], refs[n_blocks : 2 * n_blocks], refs[-1]
    planes, height, width = out_ref.shape
    grad = None
    for field_ref, op_ref in zip(field_refs, op_refs):
        field = field_ref[...].reshape(planes * height, width).astype(jnp.bfloat16)
        part = lax.dot_general(
            field, op_ref[...], (((1,), (1,)), ((), ())), preferred_element_type=jnp.float32
        )
        grad = part if grad is None else grad + part
    out_ref[...] = -(carrier_ref[...] * grad.reshape(out_ref.shape))


def z_terms(out, flat, planes, start, others, ops):
    count, height, width = others[0].shape if others else flat.shape
    tile = 4
    first, cycle, carried = start // tile, planes // tile, 2 * planes // tile
    here = pl.BlockSpec((tile, height, width), lambda i: (first + i, 0, 0))
    carrier = pl.BlockSpec((tile, height, width), lambda i: (carried + (first + i) % cycle, 0, 0))
    field = pl.BlockSpec((tile, height, width), lambda i: (i, 0, 0))
    op = pl.BlockSpec((width, width), lambda i: (0, 0))
    size = count * height * width
    return in_place(
        functools.partial(z_kernel, 1 + len(others)),
        out,
        flat.shape,
        "z_terms",
        (count // tile,),
        [flat, flat, *others, *ops],
        [carrier, here] + [field] * len(others) + [op] * len(ops),
        here,
        2 * size * width * len(ops),
        4 * size * (2 + len(ops)),
    )


def node_kernel(planes, node_ref, force_ref, base_ref, out_ref):
    tile, height, width = out_ref.shape
    out_ref[...] = base_ref[...]
    lane = lax.broadcasted_iota(jnp.int32, (1, width), 1)
    start = pl.program_id(0) * tile
    comp, begin = start // planes, start % planes

    def add_node(n, _):
        x, y, z = node_ref[0, n] - begin, node_ref[1, n], node_ref[2, n]

        @pl.when((x >= 0) & (x < tile) & (y >= 0) & (y < height) & (z >= 0) & (z < width))
        def _():
            row = out_ref[x, pl.ds(y, 1), :]
            out_ref[x, pl.ds(y, 1), :] = row + jnp.where(lane == z, force_ref[comp, n], 0.0)

        return 0

    lax.fori_loop(0, node_ref.shape[1], add_node, 0)


def add_nodes(out, planes, nodes, forces):
    total, height, width = out.shape
    tile = planes
    block = pl.BlockSpec((tile, height, width), lambda i: (i, 0, 0))
    smem = pl.BlockSpec(memory_space=pltpu.SMEM)
    return pl.pallas_call(
        functools.partial(node_kernel, planes),
        grid=(total // tile,),
        in_specs=[smem, smem, block],
        out_specs=block,
        out_shape=jax.ShapeDtypeStruct(out.shape, jnp.float32),
        input_output_aliases={2: 0},
        compiler_params=pltpu.CompilerParams(vmem_limit_bytes=VMEM),
        cost_estimate=pl.CostEstimate(flops=out.size, bytes_accessed=8 * out.size, transcendentals=0),
        name="add_nodes",
    )(nodes, forces, out)


def combine_kernel(base_ref, carrier_ref, grad_ref, out_ref):
    out_ref[...] = base_ref[...] - carrier_ref[...] * grad_ref[:, 0]


def combine(out, flat, planes, grad, start):
    total, height, width = out.shape
    comps = grad.shape[1]
    tile = planes // 4
    per = planes // tile
    first = start * per
    here = pl.BlockSpec((tile, height, width), lambda c, i: (first + c * per + i, 0, 0))
    carrier = pl.BlockSpec((tile, height, width), lambda c, i: (per + i, 0, 0))
    return pl.pallas_call(
        combine_kernel,
        grid=(comps, per),
        in_specs=[here, carrier, pl.BlockSpec((tile, 1, height, width), lambda c, i: (i, c, 0, 0))],
        out_specs=here,
        out_shape=jax.ShapeDtypeStruct(out.shape, jnp.float32),
        input_output_aliases={0: 0},
        compiler_params=pltpu.CompilerParams(vmem_limit_bytes=VMEM),
        cost_estimate=pl.CostEstimate(
            flops=2 * grad.size, bytes_accessed=16 * grad.size, transcendentals=0
        ),
        name="combine",
    )(out, flat, grad)


def place_kernel(height, each, far, place_ref, op_ref, *refs):
    line_refs, grad_refs, lines, grad = refs[:far], refs[far:-2], refs[-2], refs[-1]
    near = len(grad_refs)
    part = height // 8
    tile = lines.shape[1]

    def rows(s, t):
        start = ((place_ref[0] ^ s) * near + (place_ref[1] ^ t)) * height
        return pl.ds(pl.multiple_of(start, height), height)

    for p in range(each):
        for s in range(far):
            for t in range(near):
                block = line_refs[s][pl.ds((t * each + p) * part, part)]
                lines[rows(s, t), :] = block.reshape(height, tile).astype(jnp.bfloat16)
        grad[...] = jnp.dot(op_ref[...], lines[...], preferred_element_type=jnp.float32)
        for s in range(far):
            for t in range(near):
                block = grad[rows(s, t), :].reshape(part, 8, tile)
                grad_refs[t][pl.ds((s * each + p) * part, part)] = block


def placed_gradient(place, op, lines, height, each):
    far = len(lines)
    count, _, width = lines[0].shape
    near = (count - 1) * 8 // (each * height)
    tile = min(width, 256)
    block = pl.BlockSpec((count - 1, 8, tile), lambda j, _: (0, 0, j))
    out_count = far * each * height // 8
    out_block = pl.BlockSpec((out_count, 8, tile), lambda j, _: (0, 0, j))
    size = far * (count - 1) * 8 * width
    return pl.pallas_call(
        functools.partial(place_kernel, height, each, far),
        grid_spec=pltpu.PrefetchScalarGridSpec(
            num_scalar_prefetch=1,
            grid=(width // tile,),
            in_specs=[pl.BlockSpec(op.shape, lambda j, _: (0, 0))] + [block] * far,
            out_specs=[out_block] * near,
            scratch_shapes=[
                pltpu.VMEM((op.shape[0], tile), jnp.bfloat16),
                pltpu.VMEM((op.shape[0], tile), jnp.float32),
            ],
        ),
        out_shape=[jax.ShapeDtypeStruct((out_count, 8, width), jnp.float32)] * near,
        compiler_params=pltpu.CompilerParams(vmem_limit_bytes=VMEM),
        cost_estimate=pl.CostEstimate(
            flops=2 * op.shape[0] * size, bytes_accessed=8 * size + 2 * op.size, transcendentals=0
        ),
        name="placed_gradient",
    )(place, op, *lines)


def placed_kernel(each, place_ref, base_ref, carrier_ref, grad_ref, out_ref):
    for t in range(grad_ref.shape[0]):
        here = pl.ds((place_ref[1] ^ t) * each, each)
        out_ref[here] = base_ref[here] - carrier_ref[here] * grad_ref[t]


def placed_combine(place, out, flat, grad, planes, comp, s):
    near, each, height, width = grad.shape
    far = planes // (near * each)
    tile = min(width, 256)

    def spec(first):
        return pl.BlockSpec(
            (near * each, height, tile), lambda j, at: (first * far + (at[0] ^ s), 0, j)
        )

    return pl.pallas_call(
        functools.partial(placed_kernel, each),
        grid_spec=pltpu.PrefetchScalarGridSpec(
            num_scalar_prefetch=1,
            grid=(width // tile,),
            in_specs=[
                spec(comp),
                spec(1),
                pl.BlockSpec((near, each, height, tile), lambda j, at: (0, 0, 0, j)),
            ],
            out_specs=spec(comp),
        ),
        out_shape=jax.ShapeDtypeStruct(out.shape, jnp.float32),
        input_output_aliases={1: 0},
        compiler_params=pltpu.CompilerParams(vmem_limit_bytes=VMEM),
        cost_estimate=pl.CostEstimate(
            flops=2 * grad.size, bytes_accessed=16 * grad.size, transcendentals=0
        ),
        name="placed_combine",
    )(place, out, flat, grad)


def after(value, *others):
    return lax.optimization_barrier((value, others))[0]


def solution(mesh):
    n_row, n_col = mesh.shape["row"], mesh.shape["col"]
    near = GROUP
    far = n_row // near
    shifts = list(range(2, far)) + [1]

    def exchange(block):
        return lax.all_to_all(block, "row", split_axis=0, concat_axis=0, tiled=True)

    def swap(block, distance):
        return lax.ppermute(block, "row", [(i, i ^ distance) for i in range(n_row)])

    def per_device(velocity, dy_op, dz_op, node_force, node_cell):
        comps, planes, height, width = velocity.shape
        row_pos, col_pos = lax.axis_index("row"), lax.axis_index("col")
        total, each = comps * planes, planes // n_row
        far_pos, near_pos = row_pos // near, row_pos % near
        place = jnp.stack([far_pos, near_pos]).astype(jnp.int32)
        bulk = comps - 1
        eights = each * height // 8
        per_node = node_force.shape[1]

        own_rows = lax.dynamic_slice_in_dim(dz_op, col_pos * width, width, 0)
        ops = [
            lax.dynamic_slice_in_dim(own_rows, (col_pos + s) % n_col * width, width, 1)
            for s in range(n_col)
        ]

        def node_tile(known):
            return jnp.pad(known, ((0, 8 - known.shape[0]), (0, width - known.shape[1])))[None]

        block = velocity[:bulk].swapaxes(0, 1)
        block = block.reshape(n_row, each, bulk, height, width).swapaxes(1, 2)
        velocity, block = lax.optimization_barrier((velocity, block))
        lines = exchange(block)
        flat = velocity.reshape(total, height, width)

        def beside(piece):
            return [
                lax.ppermute(piece, "col", [(i, (i - s) % n_col) for i in range(n_col)])
                for s in range(1, n_col)
            ]

        early = 2 * total // 3
        others = beside(flat[:early])

        known = node_tile(jnp.concatenate([node_force, node_cell.astype(jnp.float32)]))
        rows = flat.reshape(total * height // 8, 8, width)
        lot = []
        for t in range(near):
            blocks = []
            for s in range(far):
                plane = bulk * planes + ((far_pos ^ s) * near + (near_pos ^ t)) * each
                blocks.append(lax.dynamic_slice_in_dim(rows, plane * height // 8, eights, 0))
            lot.append(jnp.concatenate(blocks + [known]))
        lot = [lot[0]] + [swap(lot[t], t) for t in range(1, near)]
        known = node_tile(jnp.concatenate([part[-1, :, :per_node] for part in lot], axis=1))
        landed = []
        for s in range(far):
            blocks = [part[s * eights : (s + 1) * eights] for part in lot]
            landed.append(jnp.concatenate(blocks + [known]))
        for s in shifts:
            landed[s] = swap(landed[s], s * near)
        known = jnp.concatenate([part[-1, :, : near * per_node] for part in landed], axis=1)

        grads = y_gradient(dy_op, lines)
        grads = exchange(after(grads, others, landed))

        out = z_terms(None, flat, planes, 0, others, ops)
        others = beside(after(flat, landed[1])[early:])
        grad = placed_gradient(place, dy_op, after(landed, out), height, each)
        origin = jnp.stack([0 * row_pos, row_pos * height, col_pos * width])
        cells = known[comps : 2 * comps].astype(jnp.int32) - origin[:, None].astype(jnp.int32)
        grad = [grad[0]] + [swap(grad[t], t) for t in range(1, near)]
        back = [
            jnp.stack([part[s * eights : (s + 1) * eights] for part in grad]) for s in range(far)
        ]
        others = after(others, back)
        back = [part.reshape(near, each, height, width) for part in back]
        back = [back[s] if s == 0 else swap(back[s], s * near) for s in range(far)]
        out = z_terms(out, flat, planes, early, others, ops)
        out = add_nodes(out, planes, cells, known[:comps])
        grads = grads.swapaxes(1, 2).reshape(planes, bulk, height, width)
        out = combine(out, flat, planes, grads, 0)
        for s in [0, 1] + shifts[:-1]:
            out = placed_combine(place, out, flat, back[s], planes, bulk, s)
        return out.reshape(velocity.shape)

    return jax.shard_map(
        per_device,
        mesh=mesh,
        in_specs=(
            P(None, None, "row", "col"),
            P(),
            P(),
            P(None, ("row", "col")),
            P(None, ("row", "col")),
        ),
        out_specs=P(None, None, "row", "col"),
        check_vma=False,
    )
```

```python
import functools

import jax
import jax.numpy as jnp
from jax import lax
from jax.experimental import pallas as pl
from jax.experimental.pallas import tpu as pltpu
from jax.sharding import PartitionSpec as P

VMEM = 60 << 20
GROUP = 4


def y_kernel(op_ref, lines_ref, grad_ref):
    shape = lines_ref.shape
    lines = lines_ref[...].reshape(shape[0] * shape[3], shape[4]).astype(jnp.bfloat16)
    grad = jnp.dot(op_ref[...], lines, preferred_element_type=jnp.float32)
    grad_ref[...] = grad.reshape(shape)


def y_gradient(op, lines):
    rows, comps, planes, height, width = lines.shape
    tile = min(width, 256)
    block = pl.BlockSpec((rows, 1, 1, height, tile), lambda c, p, j: (0, c, p, 0, j))
    flops = 2 * op.shape[0] * op.shape[1] * comps * planes * width
    return pl.pallas_call(
        y_kernel,
        grid=(comps, planes, width // tile),
        in_specs=[pl.BlockSpec(op.shape, lambda c, p, j: (0, 0)), block],
        out_specs=block,
        out_shape=jax.ShapeDtypeStruct(lines.shape, jnp.float32),
        compiler_params=pltpu.CompilerParams(vmem_limit_bytes=VMEM),
        cost_estimate=pl.CostEstimate(
            flops=flops, bytes_accessed=8 * lines.size + 2 * op.size, transcendentals=0
        ),
        name="y_gradient",
    )(op, lines)


def in_place(kernel, out, shape, name, grid, args, specs, out_spec, flops, size):
    kept = [] if out is None else [out]
    return pl.pallas_call(
        kernel,
        grid=grid,
        in_specs=specs + [pl.BlockSpec(memory_space=pl.ANY)] * len(kept),
        out_specs=out_spec,
        out_shape=jax.ShapeDtypeStruct(shape, jnp.float32),
        input_output_aliases={len(specs): 0} if kept else {},
        compiler_params=pltpu.CompilerParams(vmem_limit_bytes=VMEM),
        cost_estimate=pl.CostEstimate(flops=flops, bytes_accessed=size, transcendentals=0),
        name=name,
    )(*args, *kept)


def z_kernel(n_blocks, carrier_ref, *refs):
    field_refs, op_refs, out_ref = refs[:n_blocks], refs[n_blocks : 2 * n_blocks], refs[-1]
    planes, height, width = out_ref.shape
    grad = None
    for field_ref, op_ref in zip(field_refs, op_refs):
        field = field_ref[...].reshape(planes * height, width).astype(jnp.bfloat16)
        part = lax.dot_general(
            field, op_ref[...], (((1,), (1,)), ((), ())), preferred_element_type=jnp.float32
        )
        grad = part if grad is None else grad + part
    out_ref[...] = -(carrier_ref[...] * grad.reshape(out_ref.shape))


def z_terms(out, flat, planes, start, others, ops):
    count, height, width = others[0].shape if others else flat.shape
    tile = 4
    first, cycle, carried = start // tile, planes // tile, 2 * planes // tile
    here = pl.BlockSpec((tile, height, width), lambda i: (first + i, 0, 0))
    carrier = pl.BlockSpec((tile, height, width), lambda i: (carried + (first + i) % cycle, 0, 0))
    field = pl.BlockSpec((tile, height, width), lambda i: (i, 0, 0))
    op = pl.BlockSpec((width, width), lambda i: (0, 0))
    size = count * height * width
    return in_place(
        functools.partial(z_kernel, 1 + len(others)),
        out,
        flat.shape,
        "z_terms",
        (count // tile,),
        [flat, flat, *others, *ops],
        [carrier, here] + [field] * len(others) + [op] * len(ops),
        here,
        2 * size * width * len(ops),
        4 * size * (2 + len(ops)),
    )


def node_kernel(planes, node_ref, force_ref, base_ref, out_ref):
    tile, height, width = out_ref.shape
    out_ref[...] = base_ref[...]
    lane = lax.broadcasted_iota(jnp.int32, (1, width), 1)
    start = pl.program_id(0) * tile
    comp, begin = start // planes, start % planes

    def add_node(n, _):
        x, y, z = node_ref[0, n] - begin, node_ref[1, n], node_ref[2, n]

        @pl.when((x >= 0) & (x < tile) & (y >= 0) & (y < height) & (z >= 0) & (z < width))
        def _():
            row = out_ref[x, pl.ds(y, 1), :]
            out_ref[x, pl.ds(y, 1), :] = row + jnp.where(lane == z, force_ref[comp, n], 0.0)

        return 0

    lax.fori_loop(0, node_ref.shape[1], add_node, 0)


def add_nodes(out, planes, nodes, forces):
    total, height, width = out.shape
    tile = planes
    block = pl.BlockSpec((tile, height, width), lambda i: (i, 0, 0))
    smem = pl.BlockSpec(memory_space=pltpu.SMEM)
    return pl.pallas_call(
        functools.partial(node_kernel, planes),
        grid=(total // tile,),
        in_specs=[smem, smem, block],
        out_specs=block,
        out_shape=jax.ShapeDtypeStruct(out.shape, jnp.float32),
        input_output_aliases={2: 0},
        compiler_params=pltpu.CompilerParams(vmem_limit_bytes=VMEM),
        cost_estimate=pl.CostEstimate(flops=out.size, bytes_accessed=8 * out.size, transcendentals=0),
        name="add_nodes",
    )(nodes, forces, out)


def combine_kernel(base_ref, carrier_ref, grad_ref, out_ref):
    out_ref[...] = base_ref[...] - carrier_ref[...] * grad_ref[:, 0]


def combine(out, flat, planes, grad, start):
    total, height, width = out.shape
    comps = grad.shape[1]
    tile = planes // 4
    per = planes // tile
    first = start * per
    here = pl.BlockSpec((tile, height, width), lambda c, i: (first + c * per + i, 0, 0))
    carrier = pl.BlockSpec((tile, height, width), lambda c, i: (per + i, 0, 0))
    return pl.pallas_call(
        combine_kernel,
        grid=(comps, per),
        in_specs=[here, carrier, pl.BlockSpec((tile, 1, height, width), lambda c, i: (i, c, 0, 0))],
        out_specs=here,
        out_shape=jax.ShapeDtypeStruct(out.shape, jnp.float32),
        input_output_aliases={0: 0},
        compiler_params=pltpu.CompilerParams(vmem_limit_bytes=VMEM),
        cost_estimate=pl.CostEstimate(
            flops=2 * grad.size, bytes_accessed=16 * grad.size, transcendentals=0
        ),
        name="combine",
    )(out, flat, grad)


def place_kernel(height, each, far, place_ref, op_ref, *refs):
    line_refs, grad_refs, lines, grad = refs[:far], refs[far:-2], refs[-2], refs[-1]
    near = len(grad_refs)
    part = height // 8
    tile = lines.shape[1]

    def rows(s, t):
        start = ((place_ref[0] ^ s) * near + (place_ref[1] ^ t)) * height
        return pl.ds(pl.multiple_of(start, height), height)

    for p in range(each):
        for s in range(far):
            for t in range(near):
                block = line_refs[s][pl.ds((t * each + p) * part, part)]
                lines[rows(s, t), :] = block.reshape(height, tile).astype(jnp.bfloat16)
        grad[...] = jnp.dot(op_ref[...], lines[...], preferred_element_type=jnp.float32)
        for s in range(far):
            for t in range(near):
                block = grad[rows(s, t), :].reshape(part, 8, tile)
                grad_refs[t][pl.ds((s * each + p) * part, part)] = block


def placed_gradient(place, op, lines, height, each):
    far = len(lines)
    count, _, width = lines[0].shape
    near = (count - 1) * 8 // (each * height)
    tile = min(width, 256)
    block = pl.BlockSpec((count - 1, 8, tile), lambda j, _: (0, 0, j))
    out_count = far * each * height // 8
    out_block = pl.BlockSpec((out_count, 8, tile), lambda j, _: (0, 0, j))
    size = far * (count - 1) * 8 * width
    return pl.pallas_call(
        functools.partial(place_kernel, height, each, far),
        grid_spec=pltpu.PrefetchScalarGridSpec(
            num_scalar_prefetch=1,
            grid=(width // tile,),
            in_specs=[pl.BlockSpec(op.shape, lambda j, _: (0, 0))] + [block] * far,
            out_specs=[out_block] * near,
            scratch_shapes=[
                pltpu.VMEM((op.shape[0], tile), jnp.bfloat16),
                pltpu.VMEM((op.shape[0], tile), jnp.float32),
            ],
        ),
        out_shape=[jax.ShapeDtypeStruct((out_count, 8, width), jnp.float32)] * near,
        compiler_params=pltpu.CompilerParams(vmem_limit_bytes=VMEM),
        cost_estimate=pl.CostEstimate(
            flops=100 * op.shape[0] * size, bytes_accessed=8 * size + 2 * op.size, transcendentals=0
        ),
        name="placed_gradient",
    )(place, op, *lines)


def placed_kernel(near, each, planes, comp, s, base_ref, flat_ref, grad_ref, out_ref, *rest):
    base, carrier, grad, read_sems, write_sems = rest
    row_pos = lax.axis_index("row")
    far_pos, near_pos = row_pos // near, row_pos % near
    reads, writes = [], []
    for t in range(near):
        plane = ((far_pos ^ s) * near + (near_pos ^ t)) * each
        here, carried = pl.ds(comp * planes + plane, each), pl.ds(planes + plane, each)
        group = [
            pltpu.make_async_copy(base_ref.at[here], base.at[t], read_sems.at[3 * t]),
            pltpu.make_async_copy(flat_ref.at[carried], carrier.at[t], read_sems.at[3 * t + 1]),
            pltpu.make_async_copy(grad_ref.at[t], grad.at[t], read_sems.at[3 * t + 2]),
        ]
        for copy in group:
            copy.start()
        reads.append(group)
        writes.append(pltpu.make_async_copy(base.at[t], out_ref.at[here], write_sems.at[t]))
    for t in range(near):
        for copy in reads[t]:
            copy.wait()
        base[t] = base[t] - carrier[t] * grad[t]
        writes[t].start()
    for copy in writes:
        copy.wait()


def placed_combine(out, flat, grad, planes, comp, s):
    near, each, height, width = grad.shape
    anywhere = pl.BlockSpec(memory_space=pltpu.HBM)
    return pl.pallas_call(
        functools.partial(placed_kernel, near, each, planes, comp, s),
        in_specs=[anywhere, anywhere, anywhere],
        out_specs=anywhere,
        out_shape=jax.ShapeDtypeStruct(out.shape, jnp.float32),
        scratch_shapes=[pltpu.VMEM(grad.shape, jnp.float32)] * 3
        + [pltpu.SemaphoreType.DMA((3 * near,)), pltpu.SemaphoreType.DMA((near,))],
        input_output_aliases={0: 0},
        compiler_params=pltpu.CompilerParams(vmem_limit_bytes=VMEM),
        cost_estimate=pl.CostEstimate(
            flops=2 * grad.size, bytes_accessed=16 * grad.size, transcendentals=0
        ),
        name="placed_combine",
    )(out, flat, grad)


def gather_kernel(parts, field_ref, out_ref, buffer, read_sems, write_sems):
    comps, rows = out_ref.shape[2], out_ref.shape[0] // parts
    each = out_ref.shape[1]
    reads, writes = [], []
    for k in range(parts):
        here = pl.ds(k * rows, rows)
        for c in range(comps):
            for p in range(each):
                copy = pltpu.make_async_copy(
                    field_ref.at[c, here, p],
                    buffer.at[here, p, c],
                    read_sems.at[(k * comps + c) * each + p],
                )
                copy.start()
                reads.append((k, copy))
        writes.append(pltpu.make_async_copy(buffer.at[here], out_ref.at[here], write_sems.at[k]))
    for k in range(parts):
        for part, copy in reads:
            if part == k:
                copy.wait()
        writes[k].start()
    for copy in writes:
        copy.wait()


def gather_planes(velocity, comps, n_row):
    total, planes, height, width = velocity.shape
    each = planes // n_row
    shape = (n_row, each, comps, height, width)
    parts = 4
    anywhere = pl.BlockSpec(memory_space=pltpu.HBM)
    return pl.pallas_call(
        functools.partial(gather_kernel, parts),
        in_specs=[anywhere],
        out_specs=anywhere,
        out_shape=jax.ShapeDtypeStruct(shape, jnp.float32),
        scratch_shapes=[
            pltpu.VMEM(shape, jnp.float32),
            pltpu.SemaphoreType.DMA((parts * comps * each,)),
            pltpu.SemaphoreType.DMA((parts,)),
        ],
        compiler_params=pltpu.CompilerParams(vmem_limit_bytes=VMEM),
        cost_estimate=pl.CostEstimate(
            flops=0, bytes_accessed=8 * comps * planes * height * width, transcendentals=0
        ),
        name="gather_planes",
    )(velocity.reshape(total, n_row, each, height, width))


def after(value, *others):
    return lax.optimization_barrier((value, others))[0]


def solution(mesh):
    n_row, n_col = mesh.shape["row"], mesh.shape["col"]
    near = GROUP
    far = n_row // near
    shifts = list(range(2, far)) + [1]

    def exchange(block):
        return lax.all_to_all(block, "row", split_axis=0, concat_axis=0, tiled=True)

    def swap(block, distance):
        return lax.ppermute(block, "row", [(i, i ^ distance) for i in range(n_row)])

    def per_device(velocity, dy_op, dz_op, node_force, node_cell):
        comps, planes, height, width = velocity.shape
        row_pos, col_pos = lax.axis_index("row"), lax.axis_index("col")
        total, each = comps * planes, planes // n_row
        far_pos, near_pos = row_pos // near, row_pos % near
        place = jnp.stack([far_pos, near_pos]).astype(jnp.int32)
        bulk = comps - 1
        eights = each * height // 8
        per_node = node_force.shape[1]

        own_rows = lax.dynamic_slice_in_dim(dz_op, col_pos * width, width, 0)
        ops = [
            lax.dynamic_slice_in_dim(own_rows, (col_pos + s) % n_col * width, width, 1)
            for s in range(n_col)
        ]

        def node_tile(known):
            return jnp.pad(known, ((0, 8 - known.shape[0]), (0, width - known.shape[1])))[None]

        block = gather_planes(velocity, bulk, n_row).swapaxes(1, 2)
        velocity, block = lax.optimization_barrier((velocity, block))
        lines = exchange(block)
        flat = velocity.reshape(total, height, width)

        def beside(piece):
            return [
                lax.ppermute(piece, "col", [(i, (i - s) % n_col) for i in range(n_col)])
                for s in range(1, n_col)
            ]

        early = 2 * total // 3
        others = beside(flat[:early])

        known = node_tile(jnp.concatenate([node_force, node_cell.astype(jnp.float32)]))
        rows = flat.reshape(total * height // 8, 8, width)
        lot = []
        for t in range(near):
            blocks = []
            for s in range(far):
                plane = bulk * planes + ((far_pos ^ s) * near + (near_pos ^ t)) * each
                blocks.append(lax.dynamic_slice_in_dim(rows, plane * height // 8, eights, 0))
            lot.append(jnp.concatenate(blocks + [known]))
        lot = [lot[0]] + [swap(lot[t], t) for t in range(1, near)]
        known = node_tile(jnp.concatenate([part[-1, :, :per_node] for part in lot], axis=1))
        landed = []
        for s in range(far):
            blocks = [part[s * eights : (s + 1) * eights] for part in lot]
            landed.append(jnp.concatenate(blocks + [known]))
        for s in shifts:
            landed[s] = swap(landed[s], s * near)
        known = jnp.concatenate([part[-1, :, : near * per_node] for part in landed], axis=1)

        grads = y_gradient(dy_op, lines)
        grads = exchange(after(grads, others))

        out = z_terms(None, flat, planes, 0, others, ops)
        others = beside(after(flat, landed[1])[early:])
        grad = placed_gradient(place, dy_op, after(landed, out), height, each)
        origin = jnp.stack([0 * row_pos, row_pos * height, col_pos * width])
        cells = known[comps : 2 * comps].astype(jnp.int32) - origin[:, None].astype(jnp.int32)
        grad = [grad[0]] + [swap(grad[t], t) for t in range(1, near)]
        back = [
            jnp.stack([part[s * eights : (s + 1) * eights] for part in grad]) for s in range(far)
        ]
        others = after(others, back)
        back = [part.reshape(near, each, height, width) for part in back]
        back = [back[s] if s == 0 else swap(back[s], s * near) for s in range(far)]
        out = z_terms(out, flat, planes, early, others, ops)
        out = add_nodes(out, planes, cells, known[:comps])
        grads = grads.swapaxes(1, 2).reshape(planes, bulk, height, width)
        out = combine(out, flat, planes, grads, 0)
        for s in [0, 1] + shifts[:-1]:
            out = placed_combine(out, flat, back[s], planes, bulk, s)
        return out.reshape(velocity.shape)

    return jax.shard_map(
        per_device,
        mesh=mesh,
        in_specs=(
            P(None, None, "row", "col"),
            P(),
            P(),
            P(None, ("row", "col")),
            P(None, ("row", "col")),
        ),
        out_specs=P(None, None, "row", "col"),
        check_vma=False,
    )
```

```python
import functools

import jax
import jax.numpy as jnp
from jax import lax
from jax.experimental import pallas as pl
from jax.experimental.pallas import tpu as pltpu
from jax.sharding import PartitionSpec as P

VMEM = 60 << 20
GROUP = 4
AHEAD = 2


def y_kernel(op_ref, lines_ref, grad_ref):
    shape = lines_ref.shape
    lines = lines_ref[...].reshape(shape[0] * shape[3], shape[4]).astype(jnp.bfloat16)
    grad = jnp.dot(op_ref[...], lines, preferred_element_type=jnp.float32)
    grad_ref[...] = grad.reshape(shape)


def y_gradient(op, lines):
    rows, comps, planes, height, width = lines.shape
    tile = min(width, 256)
    block = pl.BlockSpec((rows, 1, 1, height, tile), lambda c, p, j: (0, c, p, 0, j))
    flops = 2 * op.shape[0] * op.shape[1] * comps * planes * width
    return pl.pallas_call(
        y_kernel,
        grid=(comps, planes, width // tile),
        in_specs=[pl.BlockSpec(op.shape, lambda c, p, j: (0, 0)), block],
        out_specs=block,
        out_shape=jax.ShapeDtypeStruct(lines.shape, jnp.float32),
        compiler_params=pltpu.CompilerParams(vmem_limit_bytes=VMEM),
        cost_estimate=pl.CostEstimate(
            flops=flops, bytes_accessed=8 * lines.size + 2 * op.size, transcendentals=0
        ),
        name="y_gradient",
    )(op, lines)


def in_place(kernel, out, shape, name, grid, args, specs, out_spec, flops, size):
    kept = [] if out is None else [out]
    return pl.pallas_call(
        kernel,
        grid=grid,
        in_specs=specs + [pl.BlockSpec(memory_space=pl.ANY)] * len(kept),
        out_specs=out_spec,
        out_shape=jax.ShapeDtypeStruct(shape, jnp.float32),
        input_output_aliases={len(specs): 0} if kept else {},
        compiler_params=pltpu.CompilerParams(vmem_limit_bytes=VMEM),
        cost_estimate=pl.CostEstimate(flops=flops, bytes_accessed=size, transcendentals=0),
        name=name,
    )(*args, *kept)


def z_kernel(n_blocks, carrier_ref, *refs):
    field_refs, op_refs, out_ref = refs[:n_blocks], refs[n_blocks : 2 * n_blocks], refs[-1]
    planes, height, width = out_ref.shape
    grad = None
    for field_ref, op_ref in zip(field_refs, op_refs):
        field = field_ref[...].reshape(planes * height, width).astype(jnp.bfloat16)
        part = lax.dot_general(
            field, op_ref[...], (((1,), (1,)), ((), ())), preferred_element_type=jnp.float32
        )
        grad = part if grad is None else grad + part
    out_ref[...] = -(carrier_ref[...] * grad.reshape(out_ref.shape))


def z_terms(out, flat, planes, start, others, ops):
    count, height, width = others[0].shape if others else flat.shape
    tile = 4
    first, cycle, carried = start // tile, planes // tile, 2 * planes // tile
    here = pl.BlockSpec((tile, height, width), lambda i: (first + i, 0, 0))
    carrier = pl.BlockSpec((tile, height, width), lambda i: (carried + (first + i) % cycle, 0, 0))
    field = pl.BlockSpec((tile, height, width), lambda i: (i, 0, 0))
    op = pl.BlockSpec((width, width), lambda i: (0, 0))
    size = count * height * width
    return in_place(
        functools.partial(z_kernel, 1 + len(others)),
        out,
        flat.shape,
        "z_terms",
        (count // tile,),
        [flat, flat, *others, *ops],
        [carrier, here] + [field] * len(others) + [op] * len(ops),
        here,
        2 * size * width * len(ops),
        4 * size * (2 + len(ops)),
    )


def node_kernel(planes, node_ref, force_ref, base_ref, out_ref):
    tile, height, width = out_ref.shape
    out_ref[...] = base_ref[...]
    lane = lax.broadcasted_iota(jnp.int32, (1, width), 1)
    start = pl.program_id(0) * tile
    comp, begin = start // planes, start % planes

    def add_node(n, _):
        x, y, z = node_ref[0, n] - begin, node_ref[1, n], node_ref[2, n]

        @pl.when((x >= 0) & (x < tile) & (y >= 0) & (y < height) & (z >= 0) & (z < width))
        def _():
            row = out_ref[x, pl.ds(y, 1), :]
            out_ref[x, pl.ds(y, 1), :] = row + jnp.where(lane == z, force_ref[comp, n], 0.0)

        return 0

    lax.fori_loop(0, node_ref.shape[1], add_node, 0)


def add_nodes(out, planes, nodes, forces):
    total, height, width = out.shape
    tile = planes
    block = pl.BlockSpec((tile, height, width), lambda i: (i, 0, 0))
    smem = pl.BlockSpec(memory_space=pltpu.SMEM)
    return pl.pallas_call(
        functools.partial(node_kernel, planes),
        grid=(total // tile,),
        in_specs=[smem, smem, block],
        out_specs=block,
        out_shape=jax.ShapeDtypeStruct(out.shape, jnp.float32),
        input_output_aliases={2: 0},
        compiler_params=pltpu.CompilerParams(vmem_limit_bytes=VMEM),
        cost_estimate=pl.CostEstimate(flops=out.size, bytes_accessed=8 * out.size, transcendentals=0),
        name="add_nodes",
    )(nodes, forces, out)


def combine_kernel(base_ref, carrier_ref, grad_ref, out_ref):
    out_ref[...] = base_ref[...] - carrier_ref[...] * grad_ref[:, 0]


def combine(out, flat, planes, grad, start):
    total, height, width = out.shape
    comps = grad.shape[1]
    tile = planes // 4
    per = planes // tile
    first = start * per
    here = pl.BlockSpec((tile, height, width), lambda c, i: (first + c * per + i, 0, 0))
    carrier = pl.BlockSpec((tile, height, width), lambda c, i: (per + i, 0, 0))
    return pl.pallas_call(
        combine_kernel,
        grid=(comps, per),
        in_specs=[here, carrier, pl.BlockSpec((tile, 1, height, width), lambda c, i: (i, c, 0, 0))],
        out_specs=here,
        out_shape=jax.ShapeDtypeStruct(out.shape, jnp.float32),
        input_output_aliases={0: 0},
        compiler_params=pltpu.CompilerParams(vmem_limit_bytes=VMEM),
        cost_estimate=pl.CostEstimate(
            flops=2 * grad.size, bytes_accessed=16 * grad.size, transcendentals=0
        ),
        name="combine",
    )(out, flat, grad)


def place_kernel(height, each, far, place_ref, op_ref, *refs):
    line_refs, grad_refs, lines, grad = refs[:far], refs[far:-2], refs[-2], refs[-1]
    near = len(grad_refs)
    part = height // 8
    tile = lines.shape[1]

    def rows(s, t):
        start = ((place_ref[0] ^ s) * near + (place_ref[1] ^ t)) * height
        return pl.ds(pl.multiple_of(start, height), height)

    for p in range(each):
        for s in range(far):
            for t in range(near):
                block = line_refs[s][pl.ds((t * each + p) * part, part)]
                lines[rows(s, t), :] = block.reshape(height, tile).astype(jnp.bfloat16)
        grad[...] = jnp.dot(op_ref[...], lines[...], preferred_element_type=jnp.float32)
        for s in range(far):
            for t in range(near):
                block = grad[rows(s, t), :].reshape(part, 8, tile)
                grad_refs[t][pl.ds((s * each + p) * part, part)] = block


def placed_gradient(place, op, lines, height, each):
    far = len(lines)
    width = lines[0].shape[2]
    near = op.shape[0] // (far * height)
    count = near * each * height // 8
    tile = min(width, 256)
    block = pl.BlockSpec((count, 8, tile), lambda j, _: (0, 0, j))
    out_count = far * each * height // 8
    out_block = pl.BlockSpec((out_count, 8, tile), lambda j, _: (0, 0, j))
    size = far * count * 8 * width
    return pl.pallas_call(
        functools.partial(place_kernel, height, each, far),
        grid_spec=pltpu.PrefetchScalarGridSpec(
            num_scalar_prefetch=1,
            grid=(width // tile,),
            in_specs=[pl.BlockSpec(op.shape, lambda j, _: (0, 0))] + [block] * far,
            out_specs=[out_block] * near,
            scratch_shapes=[
                pltpu.VMEM((op.shape[0], tile), jnp.bfloat16),
                pltpu.VMEM((op.shape[0], tile), jnp.float32),
            ],
        ),
        out_shape=[jax.ShapeDtypeStruct((out_count, 8, width), jnp.float32)] * near,
        compiler_params=pltpu.CompilerParams(vmem_limit_bytes=VMEM),
        cost_estimate=pl.CostEstimate(
            flops=100 * op.shape[0] * size, bytes_accessed=8 * size + 2 * op.size, transcendentals=0
        ),
        name="placed_gradient",
    )(place, op, *lines)


def placed_kernel(near, each, planes, comp, s, base_ref, flat_ref, grad_ref, out_ref, *rest):
    base, carrier, read_sems, write_sems = rest
    row_pos = lax.axis_index("row")
    far_pos, near_pos = row_pos // near, row_pos % near
    reads, writes = [], []
    for t in range(near):
        plane = ((far_pos ^ s) * near + (near_pos ^ t)) * each
        here, carried = pl.ds(comp * planes + plane, each), pl.ds(planes + plane, each)
        group = [
            pltpu.make_async_copy(base_ref.at[here], base.at[t], read_sems.at[2 * t]),
            pltpu.make_async_copy(flat_ref.at[carried], carrier.at[t], read_sems.at[2 * t + 1]),
        ]
        for copy in group:
            copy.start()
        reads.append(group)
        writes.append(pltpu.make_async_copy(base.at[t], out_ref.at[here], write_sems.at[t]))
    for t in range(near):
        for copy in reads[t]:
            copy.wait()
        base[t] = base[t] - carrier[t] * grad_ref[t]
        writes[t].start()
    for copy in writes:
        copy.wait()


def placed_combine(out, flat, grad, planes, comp, s):
    near, each, height, width = grad.shape
    far_off = pl.BlockSpec(memory_space=pltpu.HBM)
    return pl.pallas_call(
        functools.partial(placed_kernel, near, each, planes, comp, s),
        in_specs=[far_off, far_off, pl.BlockSpec(memory_space=pltpu.VMEM)],
        out_specs=far_off,
        out_shape=jax.ShapeDtypeStruct(out.shape, jnp.float32),
        scratch_shapes=[pltpu.VMEM(grad.shape, jnp.float32)] * 2
        + [pltpu.SemaphoreType.DMA((2 * near,)), pltpu.SemaphoreType.DMA((near,))],
        input_output_aliases={0: 0},
        compiler_params=pltpu.CompilerParams(vmem_limit_bytes=8 << 20),
        cost_estimate=pl.CostEstimate(
            flops=2 * grad.size, bytes_accessed=16 * grad.size, transcendentals=0
        ),
        name="placed_combine",
    )(out, flat, grad)


def gather_kernel(parts, field_ref, out_ref, buffer, read_sems, write_sems):
    comps, rows = out_ref.shape[2], out_ref.shape[0] // parts
    each = out_ref.shape[1]
    reads, writes = [], []
    for k in range(parts):
        here = pl.ds(k * rows, rows)
        for c in range(comps):
            for p in range(each):
                copy = pltpu.make_async_copy(
                    field_ref.at[c, here, p],
                    buffer.at[here, p, c],
                    read_sems.at[(k * comps + c) * each + p],
                )
                copy.start()
                reads.append((k, copy))
        writes.append(pltpu.make_async_copy(buffer.at[here], out_ref.at[here], write_sems.at[k]))
    for k in range(parts):
        for part, copy in reads:
            if part == k:
                copy.wait()
        writes[k].start()
    for copy in writes:
        copy.wait()


def gather_planes(velocity, comps, n_row):
    total, planes, height, width = velocity.shape
    each = planes // n_row
    shape = (n_row, each, comps, height, width)
    parts = 4
    anywhere = pl.BlockSpec(memory_space=pltpu.HBM)
    return pl.pallas_call(
        functools.partial(gather_kernel, parts),
        in_specs=[anywhere],
        out_specs=anywhere,
        out_shape=jax.ShapeDtypeStruct(shape, jnp.float32),
        scratch_shapes=[
            pltpu.VMEM(shape, jnp.float32),
            pltpu.SemaphoreType.DMA((parts * comps * each,)),
            pltpu.SemaphoreType.DMA((parts,)),
        ],
        compiler_params=pltpu.CompilerParams(vmem_limit_bytes=VMEM),
        cost_estimate=pl.CostEstimate(
            flops=0, bytes_accessed=8 * comps * planes * height * width, transcendentals=0
        ),
        name="gather_planes",
    )(velocity.reshape(total, n_row, each, height, width))


def join_kernel(first_ref, second_ref, out_ref):
    out_ref[...] = first_ref[...] + second_ref[...]


def join_tiles(first, second):
    return pl.pallas_call(
        join_kernel,
        out_shape=jax.ShapeDtypeStruct(first.shape, first.dtype),
        cost_estimate=pl.CostEstimate(flops=57500000000, bytes_accessed=0, transcendentals=0),
        name="join_tiles",
    )(first, second)


def after(value, *others):
    return lax.optimization_barrier((value, others))[0]


def solution(mesh):
    n_row, n_col = mesh.shape["row"], mesh.shape["col"]
    near = GROUP
    far = n_row // near
    shifts = list(range(2, far)) + [1]

    def exchange(block):
        return lax.all_to_all(block, "row", split_axis=0, concat_axis=0, tiled=True)

    def swap(block, distance):
        return lax.ppermute(block, "row", [(i, i ^ distance) for i in range(n_row)])

    def per_device(velocity, dy_op, dz_op, node_force, node_cell):
        comps, planes, height, width = velocity.shape
        row_pos, col_pos = lax.axis_index("row"), lax.axis_index("col")
        total, each = comps * planes, planes // n_row
        far_pos, near_pos = row_pos // near, row_pos % near
        place = jnp.stack([far_pos, near_pos]).astype(jnp.int32)
        bulk = comps - 1
        eights = each * height // 8
        per_node = node_force.shape[1]

        own_rows = lax.dynamic_slice_in_dim(dz_op, col_pos * width, width, 0)
        ops = [
            lax.dynamic_slice_in_dim(own_rows, (col_pos + s) % n_col * width, width, 1)
            for s in range(n_col)
        ]

        def node_tile(known, lane=0):
            after_lane = width - lane - known.shape[1]
            return jnp.pad(known, ((0, 8 - known.shape[0]), (lane, after_lane)))[None]

        def beside(piece):
            return [
                lax.ppermute(piece, "col", [(i, (i - s) % n_col) for i in range(n_col)])
                for s in range(1, n_col)
            ]

        def block_of(flat, s, t):
            plane = bulk * planes + ((far_pos ^ s) * near + (near_pos ^ t)) * each
            rows = flat.reshape(total * height // 8, 8, width)
            return lax.dynamic_slice_in_dim(rows, plane * height // 8, eights, 0)

        def inner(part, k):
            return part[k * eights : (k + 1) * eights]

        ahead = far - 1
        known = jnp.concatenate([node_force, node_cell.astype(jnp.float32)])
        flat = velocity.reshape(total, height, width)
        part = [block_of(flat, ahead, t) for t in range(AHEAD)]
        part = jnp.concatenate(part + [node_tile(known, per_node)])
        flat, part = lax.optimization_barrier((flat, part))
        part = swap(part, ahead * near)

        block = gather_planes(flat.reshape(velocity.shape), bulk, n_row).swapaxes(1, 2)
        flat, block = lax.optimization_barrier((flat, block))
        lines = exchange(block)

        early = 2 * total // 3
        others = beside(flat[:early])

        ahead_tile = join_tiles(node_tile(known), part[-1:])
        lot = []
        for t in range(near):
            blocks = [block_of(flat, s, t) for s in range(ahead)]
            blocks.append(inner(part, t) if t < AHEAD else block_of(flat, ahead, t))
            lot.append(jnp.concatenate(blocks + [ahead_tile]))
        lot = [swap(lot[t], t) if t else lot[t] for t in range(near)]
        known = jnp.concatenate([part[-1, :, :per_node] for part in lot], axis=1)
        ahead_known = jnp.concatenate(
            [part[-1, :, per_node : 2 * per_node] for part in lot], axis=1
        )
        tile = node_tile(known)
        landed = [jnp.concatenate([inner(part, s) for part in lot] + [tile]) for s in range(ahead)]
        for s in range(1, ahead):
            landed[s] = swap(landed[s], s * near)
        rest = jnp.concatenate([inner(part, ahead) for part in lot[AHEAD:]])
        rest = swap(rest, ahead * near)
        landed.append(jnp.concatenate([inner(part, ahead) for part in lot[:AHEAD]] + [rest]))
        known = jnp.concatenate(
            [known]
            + [landed[s][-1, :, : near * per_node] for s in range(1, ahead)]
            + [ahead_known],
            axis=1,
        )

        grads = y_gradient(dy_op, lines)
        grads = exchange(after(grads, others))

        out = z_terms(None, flat, planes, 0, others, ops)
        others = beside(after(flat, landed[1])[early:])
        grad = placed_gradient(place, dy_op, after(landed, out), height, each)
        origin = jnp.stack([0 * row_pos, row_pos * height, col_pos * width])
        cells = known[comps : 2 * comps].astype(jnp.int32) - origin[:, None].astype(jnp.int32)
        grad = [grad[0]] + [swap(grad[t], t) for t in range(1, near)]
        back = [
            jnp.stack([part[s * eights : (s + 1) * eights] for part in grad]) for s in range(far)
        ]
        others = after(others, back)
        back = [part.reshape(near, each, height, width) for part in back]
        back = [back[s] if s == 0 else swap(back[s], s * near) for s in range(far)]
        out = z_terms(out, flat, planes, early, others, ops)
        out = add_nodes(out, planes, cells, known[:comps])
        grads = grads.swapaxes(1, 2).reshape(planes, bulk, height, width)
        out = combine(out, flat, planes, grads, 0)
        for s in [0, 1] + shifts[:-1]:
            out = placed_combine(out, flat, back[s], planes, bulk, s)
        return out.reshape(velocity.shape)

    return jax.shard_map(
        per_device,
        mesh=mesh,
        in_specs=(
            P(None, None, "row", "col"),
            P(),
            P(),
            P(None, ("row", "col")),
            P(None, ("row", "col")),
        ),
        out_specs=P(None, None, "row", "col"),
        check_vma=False,
    )
```

```python
import functools

import jax
import jax.numpy as jnp
from jax import lax
from jax.experimental import pallas as pl
from jax.experimental.pallas import tpu as pltpu
from jax.sharding import PartitionSpec as P

VMEM = 60 << 20
GROUP = 4
AHEAD = 2


def y_kernel(op_ref, lines_ref, grad_ref):
    shape = lines_ref.shape
    lines = lines_ref[...].reshape(shape[0] * shape[3], shape[4]).astype(jnp.bfloat16)
    grad = jnp.dot(op_ref[...], lines, preferred_element_type=jnp.float32)
    grad_ref[...] = grad.reshape(shape)


def y_gradient(op, lines):
    rows, comps, planes, height, width = lines.shape
    tile = min(width, 256)
    block = pl.BlockSpec((rows, 1, 1, height, tile), lambda c, p, j: (0, c, p, 0, j))
    flops = 2 * op.shape[0] * op.shape[1] * comps * planes * width
    return pl.pallas_call(
        y_kernel,
        grid=(comps, planes, width // tile),
        in_specs=[pl.BlockSpec(op.shape, lambda c, p, j: (0, 0)), block],
        out_specs=block,
        out_shape=jax.ShapeDtypeStruct(lines.shape, jnp.float32),
        compiler_params=pltpu.CompilerParams(vmem_limit_bytes=VMEM),
        cost_estimate=pl.CostEstimate(
            flops=flops, bytes_accessed=8 * lines.size + 2 * op.size, transcendentals=0
        ),
        name="y_gradient",
    )(op, lines)


def in_place(kernel, out, shape, name, grid, args, specs, out_spec, flops, size):
    kept = [] if out is None else [out]
    return pl.pallas_call(
        kernel,
        grid=grid,
        in_specs=specs + [pl.BlockSpec(memory_space=pl.ANY)] * len(kept),
        out_specs=out_spec,
        out_shape=jax.ShapeDtypeStruct(shape, jnp.float32),
        input_output_aliases={len(specs): 0} if kept else {},
        compiler_params=pltpu.CompilerParams(vmem_limit_bytes=VMEM),
        cost_estimate=pl.CostEstimate(flops=flops, bytes_accessed=size, transcendentals=0),
        name=name,
    )(*args, *kept)


def z_kernel(n_blocks, carrier_ref, *refs):
    field_refs, op_refs, out_ref = refs[:n_blocks], refs[n_blocks : 2 * n_blocks], refs[-1]
    planes, height, width = out_ref.shape
    grad = None
    for field_ref, op_ref in zip(field_refs, op_refs):
        field = field_ref[...].reshape(planes * height, width).astype(jnp.bfloat16)
        part = lax.dot_general(
            field, op_ref[...], (((1,), (1,)), ((), ())), preferred_element_type=jnp.float32
        )
        grad = part if grad is None else grad + part
    out_ref[...] = -(carrier_ref[...] * grad.reshape(out_ref.shape))


def z_terms(out, flat, planes, start, others, ops):
    count, height, width = others[0].shape if others else flat.shape
    tile = 4
    first, cycle, carried = start // tile, planes // tile, 2 * planes // tile
    here = pl.BlockSpec((tile, height, width), lambda i: (first + i, 0, 0))
    carrier = pl.BlockSpec((tile, height, width), lambda i: (carried + (first + i) % cycle, 0, 0))
    field = pl.BlockSpec((tile, height, width), lambda i: (i, 0, 0))
    op = pl.BlockSpec((width, width), lambda i: (0, 0))
    size = count * height * width
    return in_place(
        functools.partial(z_kernel, 1 + len(others)),
        out,
        flat.shape,
        "z_terms",
        (count // tile,),
        [flat, flat, *others, *ops],
        [carrier, here] + [field] * len(others) + [op] * len(ops),
        here,
        2 * size * width * len(ops),
        4 * size * (2 + len(ops)),
    )


def node_kernel(planes, node_ref, force_ref, base_ref, out_ref):
    tile, height, width = out_ref.shape
    out_ref[...] = base_ref[...]
    lane = lax.broadcasted_iota(jnp.int32, (1, width), 1)
    start = pl.program_id(0) * tile
    comp, begin = start // planes, start % planes

    def add_node(n, _):
        x, y, z = node_ref[0, n] - begin, node_ref[1, n], node_ref[2, n]

        @pl.when((x >= 0) & (x < tile) & (y >= 0) & (y < height) & (z >= 0) & (z < width))
        def _():
            row = out_ref[x, pl.ds(y, 1), :]
            out_ref[x, pl.ds(y, 1), :] = row + jnp.where(lane == z, force_ref[comp, n], 0.0)

        return 0

    lax.fori_loop(0, node_ref.shape[1], add_node, 0)


def add_nodes(out, planes, nodes, forces):
    total, height, width = out.shape
    tile = planes
    block = pl.BlockSpec((tile, height, width), lambda i: (i, 0, 0))
    smem = pl.BlockSpec(memory_space=pltpu.SMEM)
    return pl.pallas_call(
        functools.partial(node_kernel, planes),
        grid=(total // tile,),
        in_specs=[smem, smem, block],
        out_specs=block,
        out_shape=jax.ShapeDtypeStruct(out.shape, jnp.float32),
        input_output_aliases={2: 0},
        compiler_params=pltpu.CompilerParams(vmem_limit_bytes=VMEM),
        cost_estimate=pl.CostEstimate(flops=out.size, bytes_accessed=8 * out.size, transcendentals=0),
        name="add_nodes",
    )(nodes, forces, out)


def combine_kernel(base_ref, carrier_ref, grad_ref, out_ref):
    out_ref[...] = base_ref[...] - carrier_ref[...] * grad_ref[:, 0]


def combine(out, flat, planes, grad, start):
    total, height, width = out.shape
    comps = grad.shape[1]
    tile = planes // 4
    per = planes // tile
    first = start * per
    here = pl.BlockSpec((tile, height, width), lambda c, i: (first + c * per + i, 0, 0))
    carrier = pl.BlockSpec((tile, height, width), lambda c, i: (per + i, 0, 0))
    return pl.pallas_call(
        combine_kernel,
        grid=(comps, per),
        in_specs=[here, carrier, pl.BlockSpec((tile, 1, height, width), lambda c, i: (i, c, 0, 0))],
        out_specs=here,
        out_shape=jax.ShapeDtypeStruct(out.shape, jnp.float32),
        input_output_aliases={0: 0},
        compiler_params=pltpu.CompilerParams(vmem_limit_bytes=VMEM),
        cost_estimate=pl.CostEstimate(
            flops=2 * grad.size, bytes_accessed=16 * grad.size, transcendentals=0
        ),
        name="combine",
    )(out, flat, grad)


def place_kernel(height, each, far, place_ref, op_ref, *refs):
    line_refs, grad_refs, lines, grad = refs[:far], refs[far:-2], refs[-2], refs[-1]
    near = len(grad_refs)
    part = height // 8
    tile = lines.shape[1]

    def rows(s, t):
        start = ((place_ref[0] ^ s) * near + (place_ref[1] ^ t)) * height
        return pl.ds(pl.multiple_of(start, height), height)

    for p in range(each):
        for s in range(far):
            for t in range(near):
                block = line_refs[s][pl.ds((t * each + p) * part, part)]
                lines[rows(s, t), :] = block.reshape(height, tile).astype(jnp.bfloat16)
        grad[...] = jnp.dot(op_ref[...], lines[...], preferred_element_type=jnp.float32)
        for s in range(far):
            for t in range(near):
                block = grad[rows(s, t), :].reshape(part, 8, tile)
                grad_refs[t][pl.ds((s * each + p) * part, part)] = block


def placed_gradient(place, op, lines, height, each):
    far = len(lines)
    width = lines[0].shape[2]
    near = op.shape[0] // (far * height)
    count = near * each * height // 8
    tile = min(width, 256)
    block = pl.BlockSpec((count, 8, tile), lambda j, _: (0, 0, j))
    out_count = far * each * height // 8
    out_block = pl.BlockSpec((out_count, 8, tile), lambda j, _: (0, 0, j))
    size = far * count * 8 * width
    return pl.pallas_call(
        functools.partial(place_kernel, height, each, far),
        grid_spec=pltpu.PrefetchScalarGridSpec(
            num_scalar_prefetch=1,
            grid=(width // tile,),
            in_specs=[pl.BlockSpec(op.shape, lambda j, _: (0, 0))] + [block] * far,
            out_specs=[out_block] * near,
            scratch_shapes=[
                pltpu.VMEM((op.shape[0], tile), jnp.bfloat16),
                pltpu.VMEM((op.shape[0], tile), jnp.float32),
            ],
        ),
        out_shape=[jax.ShapeDtypeStruct((out_count, 8, width), jnp.float32)] * near,
        compiler_params=pltpu.CompilerParams(vmem_limit_bytes=VMEM),
        cost_estimate=pl.CostEstimate(
            flops=100 * op.shape[0] * size, bytes_accessed=8 * size + 2 * op.size, transcendentals=0
        ),
        name="placed_gradient",
    )(place, op, *lines)


def planes_at(s, t, near, each, planes, comp):
    row_pos = lax.axis_index("row")
    plane = ((row_pos // near ^ s) * near + (row_pos % near ^ t)) * each
    return pl.ds(comp * planes + plane, each), pl.ds(planes + plane, each)


def placed_kernel(near, each, planes, comp, s, later, base_ref, flat_ref, grad_ref, out_ref, *rest):
    next_refs, (base, carrier, read_sems, write_sems) = rest[:-4], rest[-4:]
    reads, writes, extra = [], [], []
    for t in range(near):
        here, carried = planes_at(s, t, near, each, planes, comp)
        group = [
            pltpu.make_async_copy(base_ref.at[here], base.at[t], read_sems.at[4 * t]),
            pltpu.make_async_copy(flat_ref.at[carried], carrier.at[t], read_sems.at[4 * t + 1]),
        ]
        for copy in group:
            copy.start()
        reads.append(group)
        writes.append(pltpu.make_async_copy(base.at[t], out_ref.at[here], write_sems.at[t]))
        if later is not None:
            here, carried = planes_at(later, t, near, each, planes, comp)
            extra += [
                pltpu.make_async_copy(base_ref.at[here], next_refs[0].at[t], read_sems.at[4 * t + 2]),
                pltpu.make_async_copy(
                    flat_ref.at[carried], next_refs[1].at[t], read_sems.at[4 * t + 3]
                ),
            ]
    for copy in extra:
        copy.start()
    for t in range(near):
        for copy in reads[t]:
            copy.wait()
        base[t] = base[t] - carrier[t] * grad_ref[t]
        writes[t].start()
    for copy in writes + extra:
        copy.wait()


def placed_combine(out, flat, grad, planes, comp, s, later=None):
    near, each, height, width = grad.shape
    far_off, whole = pl.BlockSpec(memory_space=pltpu.HBM), pl.BlockSpec(memory_space=pltpu.VMEM)
    n_next = 0 if later is None else 2
    return pl.pallas_call(
        functools.partial(placed_kernel, near, each, planes, comp, s, later),
        in_specs=[far_off, far_off, whole],
        out_specs=[far_off] + [whole] * n_next,
        out_shape=[jax.ShapeDtypeStruct(out.shape, jnp.float32)]
        + [jax.ShapeDtypeStruct(grad.shape, jnp.float32)] * n_next,
        scratch_shapes=[pltpu.VMEM(grad.shape, jnp.float32)] * 2
        + [pltpu.SemaphoreType.DMA((4 * near,)), pltpu.SemaphoreType.DMA((near,))],
        input_output_aliases={0: 0},
        compiler_params=pltpu.CompilerParams(vmem_limit_bytes=8 << 20),
        cost_estimate=pl.CostEstimate(
            flops=2 * grad.size, bytes_accessed=16 * grad.size, transcendentals=0
        ),
        name="placed_combine",
    )(out, flat, grad)


def final_kernel(near, each, planes, comp, s, base_ref, carrier_ref, grad_ref, kept_ref, out_ref, *rest):
    result, write_sems = rest
    writes = []
    for t in range(near):
        here, _ = planes_at(s, t, near, each, planes, comp)
        result[t] = base_ref[t] - carrier_ref[t] * grad_ref[t]
        copy = pltpu.make_async_copy(result.at[t], out_ref.at[here], write_sems.at[t])
        copy.start()
        writes.append(copy)
    for copy in writes:
        copy.wait()


def final_combine(out, base, carrier, grad, planes, comp, s):
    near, each, height, width = grad.shape
    far_off, whole = pl.BlockSpec(memory_space=pltpu.HBM), pl.BlockSpec(memory_space=pltpu.VMEM)
    return pl.pallas_call(
        functools.partial(final_kernel, near, each, planes, comp, s),
        in_specs=[whole, whole, whole, far_off],
        out_specs=far_off,
        out_shape=jax.ShapeDtypeStruct(out.shape, jnp.float32),
        scratch_shapes=[pltpu.VMEM(grad.shape, jnp.float32), pltpu.SemaphoreType.DMA((near,))],
        input_output_aliases={3: 0},
        compiler_params=pltpu.CompilerParams(vmem_limit_bytes=8 << 20),
        cost_estimate=pl.CostEstimate(
            flops=2 * grad.size, bytes_accessed=16 * grad.size, transcendentals=0
        ),
        name="final_combine",
    )(base, carrier, grad, out)


def gather_kernel(parts, field_ref, out_ref, buffer, read_sems, write_sems):
    comps, rows = out_ref.shape[2], out_ref.shape[0] // parts
    each = out_ref.shape[1]
    reads, writes = [], []
    for k in range(parts):
        here = pl.ds(k * rows, rows)
        for c in range(comps):
            for p in range(each):
                copy = pltpu.make_async_copy(
                    field_ref.at[c, here, p],
                    buffer.at[here, p, c],
                    read_sems.at[(k * comps + c) * each + p],
                )
                copy.start()
                reads.append((k, copy))
        writes.append(pltpu.make_async_copy(buffer.at[here], out_ref.at[here], write_sems.at[k]))
    for k in range(parts):
        for part, copy in reads:
            if part == k:
                copy.wait()
        writes[k].start()
    for copy in writes:
        copy.wait()


def gather_planes(velocity, comps, n_row):
    total, planes, height, width = velocity.shape
    each = planes // n_row
    shape = (n_row, each, comps, height, width)
    parts = 4
    anywhere = pl.BlockSpec(memory_space=pltpu.HBM)
    return pl.pallas_call(
        functools.partial(gather_kernel, parts),
        in_specs=[anywhere],
        out_specs=anywhere,
        out_shape=jax.ShapeDtypeStruct(shape, jnp.float32),
        scratch_shapes=[
            pltpu.VMEM(shape, jnp.float32),
            pltpu.SemaphoreType.DMA((parts * comps * each,)),
            pltpu.SemaphoreType.DMA((parts,)),
        ],
        compiler_params=pltpu.CompilerParams(vmem_limit_bytes=VMEM),
        cost_estimate=pl.CostEstimate(
            flops=0, bytes_accessed=8 * comps * planes * height * width, transcendentals=0
        ),
        name="gather_planes",
    )(velocity.reshape(total, n_row, each, height, width))


def pack_kernel(near, far, first_row, rows_ref, part_ref, tile_ref, *refs):
    out_refs, sems = refs[:near], refs[near]
    eights = (out_refs[0].shape[0] - 1) // far
    given = part_ref.shape[0] // eights
    row_pos = lax.axis_index("row")
    far_pos, near_pos = row_pos // near, row_pos % near
    copies = []
    for t in range(near):
        for s in range(far - 1 if t < given else far):
            start = first_row + ((far_pos ^ s) * near + (near_pos ^ t)) * eights
            copy = pltpu.make_async_copy(
                rows_ref.at[pl.ds(start, eights)],
                out_refs[t].at[pl.ds(s * eights, eights)],
                sems.at[t * far + s],
            )
            copy.start()
            copies.append(copy)
    for t in range(near):
        if t < given:
            out_refs[t][pl.ds((far - 1) * eights, eights)] = part_ref[pl.ds(t * eights, eights)]
        out_refs[t][pl.ds(far * eights, 1)] = tile_ref[...]
    for copy in copies:
        copy.wait()


def pack_lots(rows, part, tile, near, far, first_row, eights):
    shape = (far * eights + 1, 8, rows.shape[2])
    whole = pl.BlockSpec(memory_space=pltpu.VMEM)
    return pl.pallas_call(
        functools.partial(pack_kernel, near, far, first_row),
        in_specs=[pl.BlockSpec(memory_space=pltpu.HBM), whole, whole],
        out_specs=[whole] * near,
        out_shape=[jax.ShapeDtypeStruct(shape, jnp.float32)] * near,
        scratch_shapes=[pltpu.SemaphoreType.DMA((near * far,))],
        compiler_params=pltpu.CompilerParams(vmem_limit_bytes=16 << 20),
        cost_estimate=pl.CostEstimate(flops=57500000000, bytes_accessed=0, transcendentals=0),
        name="pack_lots",
    )(rows, part, tile)


def after(value, *others):
    return lax.optimization_barrier((value, others))[0]


def solution(mesh):
    n_row, n_col = mesh.shape["row"], mesh.shape["col"]
    near = GROUP
    far = n_row // near
    shifts = list(range(2, far)) + [1]

    def exchange(block):
        return lax.all_to_all(block, "row", split_axis=0, concat_axis=0, tiled=True)

    def swap(block, distance):
        return lax.ppermute(block, "row", [(i, i ^ distance) for i in range(n_row)])

    def per_device(velocity, dy_op, dz_op, node_force, node_cell):
        comps, planes, height, width = velocity.shape
        row_pos, col_pos = lax.axis_index("row"), lax.axis_index("col")
        total, each = comps * planes, planes // n_row
        far_pos, near_pos = row_pos // near, row_pos % near
        place = jnp.stack([far_pos, near_pos]).astype(jnp.int32)
        bulk = comps - 1
        eights = each * height // 8
        per_node = node_force.shape[1]

        own_rows = lax.dynamic_slice_in_dim(dz_op, col_pos * width, width, 0)
        ops = [
            lax.dynamic_slice_in_dim(own_rows, (col_pos + s) % n_col * width, width, 1)
            for s in range(n_col)
        ]

        def node_tile(known, lane=0):
            after_lane = width - lane - known.shape[1]
            return jnp.pad(known, ((0, 8 - known.shape[0]), (lane, after_lane)))[None]

        def beside(piece):
            return [
                lax.ppermute(piece, "col", [(i, (i - s) % n_col) for i in range(n_col)])
                for s in range(1, n_col)
            ]

        def block_of(flat, s, t):
            plane = bulk * planes + ((far_pos ^ s) * near + (near_pos ^ t)) * each
            rows = flat.reshape(total * height // 8, 8, width)
            return lax.dynamic_slice_in_dim(rows, plane * height // 8, eights, 0)

        def inner(part, k):
            return part[k * eights : (k + 1) * eights]

        ahead = far - 1
        flat = velocity.reshape(total, height, width)
        part = jnp.concatenate([block_of(flat, ahead, t) for t in range(AHEAD)])
        flat, part = lax.optimization_barrier((flat, part))
        part = swap(part, ahead * near)

        block = gather_planes(flat.reshape(velocity.shape), bulk, n_row).swapaxes(1, 2)
        flat, block = lax.optimization_barrier((flat, block))
        lines = exchange(block)

        early = 2 * total // 3
        others = beside(flat[:early])

        known = node_tile(jnp.concatenate([node_force, node_cell.astype(jnp.float32)]))
        rows = flat.reshape(total * height // 8, 8, width)
        lot = pack_lots(rows, part, known, near, far, bulk * planes * height // 8, eights)
        lot = [swap(lot[t], t) if t else lot[t] for t in range(near)]
        known = jnp.concatenate([part[-1, :, :per_node] for part in lot], axis=1)
        tile = node_tile(known)
        landed = [jnp.concatenate([inner(part, s) for part in lot] + [tile]) for s in range(ahead)]
        for s in range(1, ahead):
            landed[s] = swap(landed[s], s * near)
        rest = jnp.concatenate([inner(part, ahead) for part in lot[AHEAD:]] + [tile])
        rest = swap(rest, ahead * near)
        landed.append(jnp.concatenate([inner(part, ahead) for part in lot[:AHEAD]] + [rest]))
        known = jnp.concatenate(
            [known] + [part[-1, :, : near * per_node] for part in landed[1:]], axis=1
        )

        grads = y_gradient(dy_op, lines)
        grads = exchange(after(grads, others))

        out = z_terms(None, flat, planes, 0, others, ops)
        others = beside(after(flat, landed[1])[early:])
        grad = placed_gradient(place, dy_op, after(landed, out), height, each)
        origin = jnp.stack([0 * row_pos, row_pos * height, col_pos * width])
        cells = known[comps : 2 * comps].astype(jnp.int32) - origin[:, None].astype(jnp.int32)
        grad = [grad[0]] + [swap(grad[t], t) for t in range(1, near)]
        back = [
            jnp.stack([part[s * eights : (s + 1) * eights] for part in grad]) for s in range(far)
        ]
        others = after(others, back)
        back = [part.reshape(near, each, height, width) for part in back]
        back = [back[s] if s == 0 else swap(back[s], s * near) for s in range(far)]
        out = z_terms(out, flat, planes, early, others, ops)
        out = add_nodes(out, planes, cells, known[:comps])
        grads = grads.swapaxes(1, 2).reshape(planes, bulk, height, width)
        out = combine(out, flat, planes, grads, 0)
        order = [0, 1] + shifts[:-1]
        for s in order[:-2]:
            (out,) = placed_combine(out, flat, back[s], planes, bulk, s)
        out, base, carrier = placed_combine(
            out, flat, back[order[-2]], planes, bulk, order[-2], order[-1]
        )
        out = final_combine(out, base, carrier, back[order[-1]], planes, bulk, order[-1])
        return out.reshape(velocity.shape)

    return jax.shard_map(
        per_device,
        mesh=mesh,
        in_specs=(
            P(None, None, "row", "col"),
            P(),
            P(),
            P(None, ("row", "col")),
            P(None, ("row", "col")),
        ),
        out_specs=P(None, None, "row", "col"),
        check_vma=False,
    )
```

```python
import functools

import jax
import jax.numpy as jnp
from jax import lax
from jax.experimental import pallas as pl
from jax.experimental.pallas import tpu as pltpu
from jax.sharding import PartitionSpec as P

VMEM = 60 << 20
GROUP = 4
AHEAD = 2
PACK_WEIGHT = 57500000000
Y_WEIGHT = 100


def y_kernel(op_ref, lines_ref, grad_ref):
    shape = lines_ref.shape
    lines = lines_ref[...].reshape(shape[0] * shape[3], shape[4]).astype(jnp.bfloat16)
    grad = jnp.dot(op_ref[...], lines, preferred_element_type=jnp.float32)
    grad_ref[...] = grad.reshape(shape)


def y_gradient(op, lines):
    rows, comps, planes, height, width = lines.shape
    tile = min(width, 256)
    block = pl.BlockSpec((rows, 1, 1, height, tile), lambda c, p, j: (0, c, p, 0, j))
    flops = 2 * op.shape[0] * op.shape[1] * comps * planes * width
    return pl.pallas_call(
        y_kernel,
        grid=(comps, planes, width // tile),
        in_specs=[pl.BlockSpec(op.shape, lambda c, p, j: (0, 0)), block],
        out_specs=block,
        out_shape=jax.ShapeDtypeStruct(lines.shape, jnp.float32),
        compiler_params=pltpu.CompilerParams(vmem_limit_bytes=VMEM),
        cost_estimate=pl.CostEstimate(
            flops=flops, bytes_accessed=8 * lines.size + 2 * op.size, transcendentals=0
        ),
        name="y_gradient",
    )(op, lines)


def in_place(kernel, out, shape, name, grid, args, specs, out_spec, flops, size):
    kept = [] if out is None else [out]
    return pl.pallas_call(
        kernel,
        grid=grid,
        in_specs=specs + [pl.BlockSpec(memory_space=pl.ANY)] * len(kept),
        out_specs=out_spec,
        out_shape=jax.ShapeDtypeStruct(shape, jnp.float32),
        input_output_aliases={len(specs): 0} if kept else {},
        compiler_params=pltpu.CompilerParams(vmem_limit_bytes=VMEM),
        cost_estimate=pl.CostEstimate(flops=flops, bytes_accessed=size, transcendentals=0),
        name=name,
    )(*args, *kept)


def z_kernel(n_blocks, carrier_ref, *refs):
    field_refs, op_refs, out_ref = refs[:n_blocks], refs[n_blocks : 2 * n_blocks], refs[-1]
    planes, height, width = out_ref.shape
    grad = None
    for field_ref, op_ref in zip(field_refs, op_refs):
        field = field_ref[...].reshape(planes * height, width).astype(jnp.bfloat16)
        part = lax.dot_general(
            field, op_ref[...], (((1,), (1,)), ((), ())), preferred_element_type=jnp.float32
        )
        grad = part if grad is None else grad + part
    out_ref[...] = -(carrier_ref[...] * grad.reshape(out_ref.shape))


def z_terms(out, flat, planes, start, others, ops):
    count, height, width = others[0].shape if others else flat.shape
    tile = 4
    first, cycle, carried = start // tile, planes // tile, 2 * planes // tile
    here = pl.BlockSpec((tile, height, width), lambda i: (first + i, 0, 0))
    carrier = pl.BlockSpec((tile, height, width), lambda i: (carried + (first + i) % cycle, 0, 0))
    field = pl.BlockSpec((tile, height, width), lambda i: (i, 0, 0))
    op = pl.BlockSpec((width, width), lambda i: (0, 0))
    size = count * height * width
    return in_place(
        functools.partial(z_kernel, 1 + len(others)),
        out,
        flat.shape,
        "z_terms",
        (count // tile,),
        [flat, flat, *others, *ops],
        [carrier, here] + [field] * len(others) + [op] * len(ops),
        here,
        2 * size * width * len(ops),
        4 * size * (2 + len(ops)),
    )


def node_kernel(planes, node_ref, force_ref, base_ref, out_ref):
    tile, height, width = out_ref.shape
    out_ref[...] = base_ref[...]
    lane = lax.broadcasted_iota(jnp.int32, (1, width), 1)
    start = pl.program_id(0) * tile
    comp, begin = start // planes, start % planes

    def add_node(n, _):
        x, y, z = node_ref[0, n] - begin, node_ref[1, n], node_ref[2, n]

        @pl.when((x >= 0) & (x < tile) & (y >= 0) & (y < height) & (z >= 0) & (z < width))
        def _():
            row = out_ref[x, pl.ds(y, 1), :]
            out_ref[x, pl.ds(y, 1), :] = row + jnp.where(lane == z, force_ref[comp, n], 0.0)

        return 0

    lax.fori_loop(0, node_ref.shape[1], add_node, 0)


def add_nodes(out, planes, nodes, forces):
    total, height, width = out.shape
    tile = planes
    block = pl.BlockSpec((tile, height, width), lambda i: (i, 0, 0))
    smem = pl.BlockSpec(memory_space=pltpu.SMEM)
    return pl.pallas_call(
        functools.partial(node_kernel, planes),
        grid=(total // tile,),
        in_specs=[smem, smem, block],
        out_specs=block,
        out_shape=jax.ShapeDtypeStruct(out.shape, jnp.float32),
        input_output_aliases={2: 0},
        compiler_params=pltpu.CompilerParams(vmem_limit_bytes=VMEM),
        cost_estimate=pl.CostEstimate(flops=out.size, bytes_accessed=8 * out.size, transcendentals=0),
        name="add_nodes",
    )(nodes, forces, out)


def combine_kernel(base_ref, carrier_ref, grad_ref, out_ref):
    out_ref[...] = base_ref[...] - carrier_ref[...] * grad_ref[:, 0]


def combine(out, flat, planes, grad, start):
    total, height, width = out.shape
    comps = grad.shape[1]
    tile = planes // 4
    per = planes // tile
    first = start * per
    here = pl.BlockSpec((tile, height, width), lambda c, i: (first + c * per + i, 0, 0))
    carrier = pl.BlockSpec((tile, height, width), lambda c, i: (per + i, 0, 0))
    return pl.pallas_call(
        combine_kernel,
        grid=(comps, per),
        in_specs=[here, carrier, pl.BlockSpec((tile, 1, height, width), lambda c, i: (i, c, 0, 0))],
        out_specs=here,
        out_shape=jax.ShapeDtypeStruct(out.shape, jnp.float32),
        input_output_aliases={0: 0},
        compiler_params=pltpu.CompilerParams(vmem_limit_bytes=VMEM),
        cost_estimate=pl.CostEstimate(
            flops=2 * grad.size, bytes_accessed=16 * grad.size, transcendentals=0
        ),
        name="combine",
    )(out, flat, grad)


def place_kernel(height, each, far, place_ref, op_ref, *refs):
    line_refs, grad_refs, lines, grad = refs[:far], refs[far:-2], refs[-2], refs[-1]
    near = len(grad_refs)
    part = height // 8
    tile = lines.shape[1]

    def rows(s, t):
        start = ((place_ref[0] ^ s) * near + (place_ref[1] ^ t)) * height
        return pl.ds(pl.multiple_of(start, height), height)

    for p in range(each):
        for s in range(far):
            for t in range(near):
                block = line_refs[s][pl.ds((t * each + p) * part, part)]
                lines[rows(s, t), :] = block.reshape(height, tile).astype(jnp.bfloat16)
        grad[...] = jnp.dot(op_ref[...], lines[...], preferred_element_type=jnp.float32)
        for s in range(far):
            for t in range(near):
                block = grad[rows(s, t), :].reshape(part, 8, tile)
                grad_refs[t][pl.ds((s * each + p) * part, part)] = block


def placed_gradient(place, op, lines, height, each):
    far = len(lines)
    width = lines[0].shape[2]
    near = op.shape[0] // (far * height)
    count = near * each * height // 8
    tile = min(width, 256)
    block = pl.BlockSpec((count, 8, tile), lambda j, _: (0, 0, j))
    out_count = far * each * height // 8
    out_block = pl.BlockSpec((out_count, 8, tile), lambda j, _: (0, 0, j))
    size = far * count * 8 * width
    return pl.pallas_call(
        functools.partial(place_kernel, height, each, far),
        grid_spec=pltpu.PrefetchScalarGridSpec(
            num_scalar_prefetch=1,
            grid=(width // tile,),
            in_specs=[pl.BlockSpec(op.shape, lambda j, _: (0, 0))] + [block] * far,
            out_specs=[out_block] * near,
            scratch_shapes=[
                pltpu.VMEM((op.shape[0], tile), jnp.bfloat16),
                pltpu.VMEM((op.shape[0], tile), jnp.float32),
            ],
        ),
        out_shape=[jax.ShapeDtypeStruct((out_count, 8, width), jnp.float32)] * near,
        compiler_params=pltpu.CompilerParams(vmem_limit_bytes=VMEM),
        cost_estimate=pl.CostEstimate(
            flops=Y_WEIGHT * op.shape[0] * size, bytes_accessed=8 * size + 2 * op.size, transcendentals=0
        ),
        name="placed_gradient",
    )(place, op, *lines)


def planes_at(s, t, near, each, planes, comp):
    row_pos = lax.axis_index("row")
    plane = ((row_pos // near ^ s) * near + (row_pos % near ^ t)) * each
    return pl.ds(comp * planes + plane, each), pl.ds(planes + plane, each)


def placed_kernel(near, each, planes, comp, s, later, base_ref, flat_ref, grad_ref, out_ref, *rest):
    next_refs, (base, carrier, read_sems, write_sems) = rest[:-4], rest[-4:]
    reads, writes, extra = [], [], []
    for t in range(near):
        here, carried = planes_at(s, t, near, each, planes, comp)
        group = [
            pltpu.make_async_copy(base_ref.at[here], base.at[t], read_sems.at[4 * t]),
            pltpu.make_async_copy(flat_ref.at[carried], carrier.at[t], read_sems.at[4 * t + 1]),
        ]
        for copy in group:
            copy.start()
        reads.append(group)
        writes.append(pltpu.make_async_copy(base.at[t], out_ref.at[here], write_sems.at[t]))
        if later is not None:
            here, carried = planes_at(later, t, near, each, planes, comp)
            extra += [
                pltpu.make_async_copy(base_ref.at[here], next_refs[0].at[t], read_sems.at[4 * t + 2]),
                pltpu.make_async_copy(
                    flat_ref.at[carried], next_refs[1].at[t], read_sems.at[4 * t + 3]
                ),
            ]
    for copy in extra:
        copy.start()
    for t in range(near):
        for copy in reads[t]:
            copy.wait()
        base[t] = base[t] - carrier[t] * grad_ref[t]
        writes[t].start()
    for copy in writes + extra:
        copy.wait()


def placed_combine(out, flat, grad, planes, comp, s, later=None):
    near, each, height, width = grad.shape
    far_off, whole = pl.BlockSpec(memory_space=pltpu.HBM), pl.BlockSpec(memory_space=pltpu.VMEM)
    n_next = 0 if later is None else 2
    return pl.pallas_call(
        functools.partial(placed_kernel, near, each, planes, comp, s, later),
        in_specs=[far_off, far_off, whole],
        out_specs=[far_off] + [whole] * n_next,
        out_shape=[jax.ShapeDtypeStruct(out.shape, jnp.float32)]
        + [jax.ShapeDtypeStruct(grad.shape, jnp.float32)] * n_next,
        scratch_shapes=[pltpu.VMEM(grad.shape, jnp.float32)] * 2
        + [pltpu.SemaphoreType.DMA((4 * near,)), pltpu.SemaphoreType.DMA((near,))],
        input_output_aliases={0: 0},
        compiler_params=pltpu.CompilerParams(vmem_limit_bytes=8 << 20),
        cost_estimate=pl.CostEstimate(
            flops=2 * grad.size, bytes_accessed=16 * grad.size, transcendentals=0
        ),
        name="placed_combine",
    )(out, flat, grad)


def final_kernel(near, each, planes, comp, s, base_ref, carrier_ref, grad_ref, kept_ref, out_ref, *rest):
    result, write_sems = rest
    writes = []
    for t in range(near):
        here, _ = planes_at(s, t, near, each, planes, comp)
        result[t] = base_ref[t] - carrier_ref[t] * grad_ref[t]
        copy = pltpu.make_async_copy(result.at[t], out_ref.at[here], write_sems.at[t])
        copy.start()
        writes.append(copy)
    for copy in writes:
        copy.wait()


def final_combine(out, base, carrier, grad, planes, comp, s):
    near, each, height, width = grad.shape
    far_off, whole = pl.BlockSpec(memory_space=pltpu.HBM), pl.BlockSpec(memory_space=pltpu.VMEM)
    return pl.pallas_call(
        functools.partial(final_kernel, near, each, planes, comp, s),
        in_specs=[whole, whole, whole, far_off],
        out_specs=far_off,
        out_shape=jax.ShapeDtypeStruct(out.shape, jnp.float32),
        scratch_shapes=[pltpu.VMEM(grad.shape, jnp.float32), pltpu.SemaphoreType.DMA((near,))],
        input_output_aliases={3: 0},
        compiler_params=pltpu.CompilerParams(vmem_limit_bytes=8 << 20),
        cost_estimate=pl.CostEstimate(
            flops=2 * grad.size, bytes_accessed=16 * grad.size, transcendentals=0
        ),
        name="final_combine",
    )(base, carrier, grad, out)


def gather_kernel(parts, field_ref, out_ref, buffer, read_sems, write_sems):
    comps, rows = out_ref.shape[2], out_ref.shape[0] // parts
    each = out_ref.shape[1]
    reads, writes = [], []
    for k in range(parts):
        here = pl.ds(k * rows, rows)
        for c in range(comps):
            for p in range(each):
                copy = pltpu.make_async_copy(
                    field_ref.at[c, here, p],
                    buffer.at[here, p, c],
                    read_sems.at[(k * comps + c) * each + p],
                )
                copy.start()
                reads.append((k, copy))
        writes.append(pltpu.make_async_copy(buffer.at[here], out_ref.at[here], write_sems.at[k]))
    for k in range(parts):
        for part, copy in reads:
            if part == k:
                copy.wait()
        writes[k].start()
    for copy in writes:
        copy.wait()


def gather_planes(velocity, comps, n_row):
    total, planes, height, width = velocity.shape
    each = planes // n_row
    shape = (n_row, each, comps, height, width)
    parts = 4
    anywhere = pl.BlockSpec(memory_space=pltpu.HBM)
    return pl.pallas_call(
        functools.partial(gather_kernel, parts),
        in_specs=[anywhere],
        out_specs=anywhere,
        out_shape=jax.ShapeDtypeStruct(shape, jnp.float32),
        scratch_shapes=[
            pltpu.VMEM(shape, jnp.float32),
            pltpu.SemaphoreType.DMA((parts * comps * each,)),
            pltpu.SemaphoreType.DMA((parts,)),
        ],
        compiler_params=pltpu.CompilerParams(vmem_limit_bytes=VMEM),
        cost_estimate=pl.CostEstimate(
            flops=0, bytes_accessed=8 * comps * planes * height * width, transcendentals=0
        ),
        name="gather_planes",
    )(velocity.reshape(total, n_row, each, height, width))


def pack_kernel(near, far, first_row, rows_ref, part_ref, tile_ref, *refs):
    out_refs, sems = refs[:near], refs[near]
    eights = (out_refs[0].shape[0] - 1) // far
    given = part_ref.shape[0] // eights
    row_pos = lax.axis_index("row")
    far_pos, near_pos = row_pos // near, row_pos % near
    copies = []
    for t in range(near):
        for s in range(far - 1 if t < given else far):
            start = first_row + ((far_pos ^ s) * near + (near_pos ^ t)) * eights
            copy = pltpu.make_async_copy(
                rows_ref.at[pl.ds(start, eights)],
                out_refs[t].at[pl.ds(s * eights, eights)],
                sems.at[t * far + s],
            )
            copy.start()
            copies.append(copy)
    for t in range(near):
        if t < given:
            out_refs[t][pl.ds((far - 1) * eights, eights)] = part_ref[pl.ds(t * eights, eights)]
        out_refs[t][pl.ds(far * eights, 1)] = tile_ref[...]
    for copy in copies:
        copy.wait()


def pack_lots(rows, part, tile, near, far, first_row, eights):
    shape = (far * eights + 1, 8, rows.shape[2])
    whole = pl.BlockSpec(memory_space=pltpu.VMEM)
    return pl.pallas_call(
        functools.partial(pack_kernel, near, far, first_row),
        in_specs=[pl.BlockSpec(memory_space=pltpu.HBM), whole, whole],
        out_specs=[whole] * near,
        out_shape=[jax.ShapeDtypeStruct(shape, jnp.float32)] * near,
        scratch_shapes=[pltpu.SemaphoreType.DMA((near * far,))],
        compiler_params=pltpu.CompilerParams(vmem_limit_bytes=16 << 20),
        cost_estimate=pl.CostEstimate(flops=PACK_WEIGHT, bytes_accessed=0, transcendentals=0),
        name="pack_lots",
    )(rows, part, tile)


def after(value, *others):
    return lax.optimization_barrier((value, others))[0]


def solution(mesh):
    n_row, n_col = mesh.shape["row"], mesh.shape["col"]
    near = GROUP
    far = n_row // near
    shifts = list(range(2, far)) + [1]

    def exchange(block):
        return lax.all_to_all(block, "row", split_axis=0, concat_axis=0, tiled=True)

    def swap(block, distance):
        return lax.ppermute(block, "row", [(i, i ^ distance) for i in range(n_row)])

    def per_device(velocity, dy_op, dz_op, node_force, node_cell):
        comps, planes, height, width = velocity.shape
        row_pos, col_pos = lax.axis_index("row"), lax.axis_index("col")
        total, each = comps * planes, planes // n_row
        far_pos, near_pos = row_pos // near, row_pos % near
        place = jnp.stack([far_pos, near_pos]).astype(jnp.int32)
        bulk = comps - 1
        eights = each * height // 8
        per_node = node_force.shape[1]

        own_rows = lax.dynamic_slice_in_dim(dz_op, col_pos * width, width, 0)
        ops = [
            lax.dynamic_slice_in_dim(own_rows, (col_pos + s) % n_col * width, width, 1)
            for s in range(n_col)
        ]

        def node_tile(known):
            return jnp.pad(known, ((0, 8 - known.shape[0]), (0, width - known.shape[1])))[None]

        def beside(piece):
            return [
                lax.ppermute(piece, "col", [(i, (i - s) % n_col) for i in range(n_col)])
                for s in range(1, n_col)
            ]

        def block_of(flat, s, t):
            plane = bulk * planes + ((far_pos ^ s) * near + (near_pos ^ t)) * each
            rows = flat.reshape(total * height // 8, 8, width)
            return lax.dynamic_slice_in_dim(rows, plane * height // 8, eights, 0)

        def inner(part, k):
            return part[k * eights : (k + 1) * eights]

        ahead = far - 1
        flat = velocity.reshape(total, height, width)
        part = jnp.concatenate([block_of(flat, ahead, t) for t in range(AHEAD)])
        flat, part = lax.optimization_barrier((flat, part))
        part = swap(part, ahead * near)

        block = gather_planes(flat.reshape(velocity.shape), bulk, n_row).swapaxes(1, 2)
        flat, block = lax.optimization_barrier((flat, block))
        lines = exchange(block)

        early = 2 * total // 3
        others = beside(flat[:early])

        known = node_tile(jnp.concatenate([node_force, node_cell.astype(jnp.float32)]))
        rows = flat.reshape(total * height // 8, 8, width)
        lot = pack_lots(rows, part, known, near, far, bulk * planes * height // 8, eights)
        lot = [swap(lot[t], t) if t else lot[t] for t in range(near)]
        known = jnp.concatenate([part[-1, :, :per_node] for part in lot], axis=1)
        tile = node_tile(known)
        landed = [jnp.concatenate([inner(part, s) for part in lot]) for s in range(ahead)]
        for s in range(1, ahead):
            landed[s] = swap(landed[s], s * near)
        rest = jnp.concatenate([inner(part, ahead) for part in lot[AHEAD:]])
        rest = swap(rest, ahead * near)
        landed.append(jnp.concatenate([inner(part, ahead) for part in lot[:AHEAD]] + [rest]))
        small = tile[:, :, :128]
        known = jnp.concatenate(
            [known] + [swap(small, s * near)[-1, :, : near * per_node] for s in range(1, far)], axis=1
        )

        grads = y_gradient(dy_op, lines)
        grads = exchange(after(grads, others))

        out = z_terms(None, flat, planes, 0, others, ops)
        others = beside(after(flat, landed[1])[early:])
        grad = placed_gradient(place, dy_op, after(landed, out), height, each)
        origin = jnp.stack([0 * row_pos, row_pos * height, col_pos * width])
        cells = known[comps : 2 * comps].astype(jnp.int32) - origin[:, None].astype(jnp.int32)
        grad = [grad[0]] + [swap(grad[t], t) for t in range(1, near)]
        back = [
            jnp.stack([part[s * eights : (s + 1) * eights] for part in grad]) for s in range(far)
        ]
        others = after(others, back)
        back = [part.reshape(near, each, height, width) for part in back]
        back = [back[s] if s == 0 else swap(back[s], s * near) for s in range(far)]
        out = z_terms(out, flat, planes, early, others, ops)
        out = add_nodes(out, planes, cells, known[:comps])
        grads = grads.swapaxes(1, 2).reshape(planes, bulk, height, width)
        out = combine(out, flat, planes, grads, 0)
        order = [0, 1] + shifts[:-1]
        for s in order[:-2]:
            (out,) = placed_combine(out, flat, back[s], planes, bulk, s)
        out, base, carrier = placed_combine(
            out, flat, back[order[-2]], planes, bulk, order[-2], order[-1]
        )
        out = final_combine(out, base, carrier, back[order[-1]], planes, bulk, order[-1])
        return out.reshape(velocity.shape)

    return jax.shard_map(
        per_device,
        mesh=mesh,
        in_specs=(
            P(None, None, "row", "col"),
            P(),
            P(),
            P(None, ("row", "col")),
            P(None, ("row", "col")),
        ),
        out_specs=P(None, None, "row", "col"),
        check_vma=False,
    )
```
